32 devices in a mesh: ty: 4 (over z), tx: 8 (over y, x, core).
Axes of the slice: x: 2, y: 2, z: 4, core: 2. Of those that a mesh axis runs over, the one named last changes fastest.
Arguments:
- observed: float32 [6, 512, 2048], P(None, 'ty', 'tx'), may hold values from -6 to 6
- inverse_variance: float32 [6, 512, 2048], P(None, 'ty', 'tx'), may hold values from 0.5 to 4
- sed: float32 [4, 8, 6], P('ty', 'tx'), may hold values from 0.2 to 2
- morph: float32 [4, 8, 128, 128], P('ty', 'tx'), may hold values from 0.02 to 1
- foot_block: int32 [4, 8], P('ty', 'tx'), may hold values from 0 to 15, as said below
- gamma: float32 [4, 8], P('ty', 'tx'), may hold values from 0.3 to 1.5
- row_kernel: float32 [6, 41], replicated, may hold values from -1 to 1
- col_kernel: float32 [6, 41], replicated, may hold values from -1 to 1
Outputs:
- residual: float32 [6, 512, 2048], P(None, 'ty', 'tx')
- new_morph: float32 [4, 8, 128, 128], P('ty', 'tx')
- new_sed: float32 [4, 8, 6], P('ty', 'tx')
The draws below stay inside these ranges and needn't reach their ends.
Inputs may be any that keep to these rules, and one draw needn't show every extreme that they name: A source's footprint lies in its own tile row, at box column foot_block counted over the whole row; in every tile row at most 2 sources lie in one tile of 2 box columns, and some tile holds exactly 2.
All inputs are finite; a program needn't handle non-finite values.
Results may differ from the reference program's by a relative error of at most 0.0003.
Values sent between devices are 32-bit elements; how exact they have to be, the bound alone decides.
No kernel may reach another device: no remote copies, remote signals or barrier semaphores. Data moves between devices by JAX's collectives and lax.ppermute only.
A program may use at most 64 MiB of HBM per device.

```python
import math
import jax
import jax.numpy as jnp
from jax import lax

BANDS = 6
FOOT = 128
TAPS = 41
BPT = 2
S_DEV = 1
SOURCES_ROW = 8
TROWS = 4
HEIGHT = 512
WIDTH = 2048
N_TY = 4
N_TX = 8


def draw_foot_block(key, part):
    tiles = SOURCES_ROW // S_DEV
    slots_tile = 2 * S_DEV
    total = tiles * slots_tile

    def one_row(index):
        row_key = jax.random.fold_in(jax.random.fold_in(key, 7103), index)
        key_rank, key_tile, key_order, key_box = jax.random.split(row_key, 4)
        ranking = jax.random.permutation(key_rank, total).astype(jnp.int32)
        chosen = jax.random.randint(key_tile, (), 0, tiles, dtype=jnp.int32)
        slot_ids = jnp.arange(total, dtype=jnp.int32)
        scores = ranking - total * (slot_ids // slots_tile == chosen).astype(jnp.int32)
        order = jnp.argsort(scores, stable=True)[:SOURCES_ROW].astype(jnp.int32)
        shuffle = jax.random.permutation(key_order, SOURCES_ROW).astype(jnp.int32)
        slot_of = order[shuffle]
        tile_of = slot_of // slots_tile
        offset = jax.random.randint(key_box, (SOURCES_ROW,), 0, BPT, dtype=jnp.int32)
        return tile_of * BPT + offset
    return jax.vmap(one_row)(jnp.arange(TROWS, dtype=jnp.int32))


def levels(rng, extent, cuts, least, high):
    factor_of = 1.0
    for position, blocks in cuts:
        draws = jax.random.uniform(jax.random.fold_in(jax.random.fold_in(rng, 6), position), (blocks,), jnp.float32, least / len(cuts), high / len(cuts))
        factor_of = factor_of * jnp.repeat(jnp.exp(draws), extent[position] // blocks).reshape((-1,) + (1,) * (len(extent) - 1 - position))
    return factor_of


def scatter_about(own_key, shape, width, most, cuts=(), kind=jnp.bfloat16):
    values = jax.random.normal(own_key, shape, jnp.float32) * width
    if len(cuts) > 0:
        values = levels(own_key, shape, cuts, -0.22, 0.18) * values
    return jnp.clip(values, min=-most, max=most).astype(kind)


def setup_inputs(seed: int = 0) -> dict:
    splits = jax.random.split(jax.random.key(seed), 9)
    observed = scatter_about(splits[0], (BANDS, HEIGHT, WIDTH), 1.0, 6.0, ((1, 4), (2, 8)), jnp.float32)
    inverse_variance = jnp.clip(jnp.exp(math.log(4.0) - 2.0794415 * jax.random.uniform(splits[1], (BANDS, HEIGHT, WIDTH), jnp.float32) ** levels(splits[1], (BANDS, HEIGHT, WIDTH), ((1, 4), (2, 8)), -0.2, 0.2)), 0.5, 4.0)
    sed = jnp.clip(jnp.exp(math.log(2.0) - 2.3025851 * jax.random.uniform(splits[2], (TROWS, SOURCES_ROW, BANDS), jnp.float32) ** levels(splits[2], (TROWS, SOURCES_ROW, BANDS), ((0, 4), (1, 8)), -0.2, 0.2)), 0.2, 2.0)
    morph = jnp.clip(jnp.exp(math.log(1.0) - 3.912023 * jax.random.uniform(splits[3], (TROWS, SOURCES_ROW, FOOT, FOOT), jnp.float32) ** levels(splits[3], (TROWS, SOURCES_ROW, FOOT, FOOT), ((0, 4), (1, 8)), -0.2, 0.2)), 0.02, 1.0)
    foot_block = draw_foot_block(jax.random.fold_in(splits[8], 71), 0)
    gamma = jnp.clip(jnp.exp(math.log(1.5) - 1.60943787 * jax.random.uniform(splits[5], (TROWS, SOURCES_ROW), jnp.float32) ** levels(splits[5], (TROWS, SOURCES_ROW), ((0, 4), (1, 8)), -0.2, 0.2)), 0.3, 1.5)
    row_kernel = scatter_about(splits[6], (BANDS, TAPS), TAPS ** -0.5, 1.0, (), jnp.float32)
    col_kernel = scatter_about(splits[7], (BANDS, TAPS), TAPS ** -0.5, 1.0, (), jnp.float32)
    return dict(observed=observed, inverse_variance=inverse_variance, sed=sed, morph=morph, foot_block=foot_block, gamma=gamma, row_kernel=row_kernel, col_kernel=col_kernel)


HIGHEST_PRECISION = lax.Precision.HIGHEST

def band_pass(items):
    image, seen, weights, krow, kcol = items
    reach = (krow.shape[0] - 1) // 2
    lhs = image[None, None]
    blurred = lax.conv_general_dilated(lhs, kcol[::-1][None, None, None, :], (1, 1), ((0, 0), (reach, reach)), precision=HIGHEST_PRECISION)
    predicted = lax.conv_general_dilated(blurred, krow[::-1][None, None, :, None], (1, 1), ((reach, reach), (0, 0)), precision=HIGHEST_PRECISION)
    resid = weights * (seen - predicted[0, 0])
    backrows = lax.conv_general_dilated(resid[None, None], krow[None, None, :, None], (1, 1), ((reach, reach), (0, 0)), precision=HIGHEST_PRECISION)
    gradient = lax.conv_general_dilated(backrows, kcol[None, None, None, :], (1, 1), ((0, 0), (reach, reach)), precision=HIGHEST_PRECISION)
    return (resid, gradient[0, 0])

def reference(observed, inverse_variance, sed, morph, foot_block, gamma, row_kernel, col_kernel):
    blocks = BPT * N_TX
    placed = (foot_block[:, :, None] == jnp.arange(blocks, dtype=jnp.int32)[None, None, :]).astype(jnp.float32)
    weighted = placed[:, :, None, :] * sed[:, :, :, None]

    def render(items):
        weighted_row, morph_row = items
        return jnp.einsum('kbj,krc->brjc', weighted_row, morph_row, precision=HIGHEST_PRECISION)
    model = lax.map(render, (weighted, morph))
    model = model.transpose(1, 0, 2, 3, 4).reshape(BANDS, N_TY * FOOT, blocks * FOOT)
    residual, gradient = lax.map(band_pass, (model, observed, inverse_variance, row_kernel, col_kernel))
    grid = gradient.reshape(BANDS, N_TY, FOOT, blocks, FOOT).transpose(1, 0, 2, 3, 4)

    def source_terms(items):
        weighted_row, placed_row, morph_row, grid_row = items
        morph_terms = jnp.einsum('kbj,brjc->krc', weighted_row, grid_row, precision=HIGHEST_PRECISION)
        raw_terms = jnp.einsum('krc,brjc->kbj', morph_row, grid_row, precision=HIGHEST_PRECISION)
        sed_terms = lax.optimization_barrier(jnp.sum(raw_terms * placed_row[:, None, :], axis=2))
        return (morph_terms, sed_terms)
    morph_grad, sed_grad = lax.map(source_terms, (weighted, placed, morph, grid))
    step_morph = gamma / lax.optimization_barrier(jnp.sum(sed * sed, axis=2))
    new_morph = jnp.maximum(morph + step_morph[:, :, None, None] * morph_grad, 0.0)
    step_sed = gamma / jnp.sqrt(lax.optimization_barrier(jnp.sum(morph * morph, axis=(2, 3))))
    new_sed = jnp.maximum(sed + step_sed[:, :, None] * sed_grad, 0.0)
    return (residual, new_morph, new_sed)
```

```python
import functools

import jax
import jax.numpy as jnp
from jax import lax
from jax.experimental import pallas as pl
from jax.experimental.pallas import tpu as pltpu
from jax.sharding import PartitionSpec as P

F32 = jnp.float32
BF16 = jnp.bfloat16
VMEM = pl.BlockSpec(memory_space=pltpu.VMEM)
SMEM = pl.BlockSpec(memory_space=pltpu.SMEM)
HBM = pl.BlockSpec(memory_space=pl.ANY)
LIMIT = 32 * 1024 * 1024


def up_to(value, step):
    return -(-value // step) * step


def halves(value):
    high = value.astype(BF16)
    return high, (value - high.astype(F32)).astype(BF16)


def product(left, right, transposed=False):
    dims = (((1,), (1 if transposed else 0,)), ((), ()))
    dot = functools.partial(lax.dot_general, dimension_numbers=dims, preferred_element_type=F32)
    (lh, ll), (rh, rl) = left, right
    return dot(lh, rh) + (dot(lh, rl) + dot(ll, rh))


def bands_kernel(shape, row_ref, flip_ref, col_ref, cols_h, cols_l, rows_h, rows_l, back_h, back_l):
    rows, cols, box, reach, halo, rim = shape
    width = col_ref.shape[1]

    def toeplitz(ref, band, count, shift):
        placed = pltpu.roll(jnp.broadcast_to(ref[band : band + 1, :], (8, width)), shift % width, 1)
        spread = jnp.broadcast_to(placed[:1, :], (count, width))
        return pltpu.roll(spread, 0, 1, stride=1, stride_axis=0)

    def keep(high, low, band, start, value):
        h, l = halves(value)
        high[band, start : start + value.shape[0], :] = h
        low[band, start : start + value.shape[0], :] = l

    lower = lax.broadcasted_iota(jnp.int32, (box, cols), 0) >= box // 2
    for band in range(cols_h.shape[0]):
        keep(cols_h, cols_l, band, 0, toeplitz(col_ref, band, cols, -reach)[:, :cols])
        left = toeplitz(col_ref, band, box, -box - reach)[:, :cols]
        right = toeplitz(col_ref, band, box, cols - reach)[:, :cols]
        keep(cols_h, cols_l, band, cols, jnp.where(lower, left, right))
        tall = rows + 2 * rim
        wide = rows + 2 * halo
        keep(rows_h, rows_l, band, 0, toeplitz(flip_ref, band, wide, rim - halo - reach)[:, :tall])
        keep(back_h, back_l, band, 0, toeplitz(row_ref, band, rows, halo - reach)[:, :wide])


def band_matrices(row_kernel, col_kernel, shape):
    rows, cols, box, reach, halo, rim = shape
    bands, taps = row_kernel.shape
    width = up_to(cols + 2 * box + taps, 128)
    pad = lambda kernel: jnp.pad(kernel, ((0, 0), (0, width - taps)))
    sizes = [(cols + box, cols), (rows + 2 * halo, rows + 2 * rim), (rows, rows + 2 * halo)]
    return pl.pallas_call(
        functools.partial(bands_kernel, shape),
        out_shape=[jax.ShapeDtypeStruct((bands,) + s, BF16) for s in sizes for _ in range(2)],
        in_specs=[VMEM] * 3,
        out_specs=[VMEM] * 6,
        compiler_params=pltpu.CompilerParams(vmem_limit_bytes=LIMIT),
        name="band_matrices",
    )(pad(row_kernel), pad(row_kernel[:, ::-1]), pad(col_kernel))


def main_kernel(
    shape,
    place,
    same,
    other,
    above,
    below,
    halo_above,
    halo_below,
    observed_hbm,
    weights_hbm,
    cols_h,
    cols_l,
    rows_h,
    rows_l,
    back_h,
    back_l,
    residual_hbm,
    terms_same,
    terms_other,
    observed,
    weights,
    residual,
    model,
    sems,
):
    rows, cols, box, reach, halo, rim = shape
    bands = observed.shape[0]
    loads = [
        [
            pltpu.make_async_copy(hbm.at[band], vmem.at[band], sems.at[index, band])
            for index, (hbm, vmem) in enumerate(((observed_hbm, observed), (weights_hbm, weights)))
        ]
        for band in range(bands)
    ]
    for pair in loads:
        for copy in pair:
            copy.start()
    per_tile = cols // box
    half = same.shape[0]
    count = 2 * half
    first = place[0].astype(F32)
    lane = lax.broadcasted_iota(jnp.int32, (count, box), 1)

    def spread(info, index):
        return jnp.broadcast_to(info[:, index : index + 1], info.shape)

    def placed(info):
        foot = spread(info, bands) - first
        edge = jnp.where(lane >= box // 2, -1.0, float(per_tile))
        return [(foot == column).astype(F32) for column in (*map(float, range(per_tile)), edge)]

    own_info = jnp.concatenate([ref[k, box : box + 1, :] for ref in (same, other) for k in range(half)], 0)
    above_info = jnp.concatenate([above[k, rim : rim + 1, :] for k in range(count)], 0)
    below_info = jnp.concatenate([below[k, rim : rim + 1, :] for k in range(count)], 0)
    above_info = jnp.where(place[1] > 0, above_info, 0.0)
    below_info = jnp.where(place[2] > 0, below_info, 0.0)
    parts = (
        (above_info, placed(above_info), 0, rim, lambda k: above[k, :rim, :]),
        (own_info, placed(own_info), rim, rows, lambda k: (same if k < half else other)[k % half, :box, :]),
        (below_info, placed(below_info), rim + rows, rim, lambda k: below[k, :rim, :]),
    )
    own_placed = parts[1][1]
    stores = []
    for band in range(bands):
        for info, where, start, length, source in parts:
            seds = spread(info, band)
            for j, mask in enumerate(where):
                weight = mask * seds
                total = weight[0:1, :] * source(0)
                for k in range(1, count):
                    total += weight[k : k + 1, :] * source(k)
                model[start : start + length, j * box : (j + 1) * box] = total
        matrix = (cols_h[band], cols_l[band])
        blurred = product(halves(model[...]), matrix)
        predicted = product((rows_h[band], rows_l[band]), halves(blurred))
        for copy in loads[band]:
            copy.wait()
        own = weights[band] * (observed[band] - predicted[halo : halo + rows])
        residual[band] = own
        store = pltpu.make_async_copy(residual.at[band], residual_hbm.at[band], sems.at[2, band])
        store.start()
        stores.append(store)
        before = halo_above[bands + band] * (halo_above[band] - predicted[:halo])
        after = halo_below[bands + band] * (halo_below[band] - predicted[halo + rows :])
        tall = jnp.concatenate([before, own, after], 0)
        backrows = product((back_h[band], back_l[band]), halves(tall))
        gradient = product(halves(backrows), matrix, transposed=True)
        seds = spread(own_info, band)
        for k in range(count):
            terms = terms_same if k < half else terms_other
            at = k % half
            mine = own_placed[0][k : k + 1, :] * gradient[:, :box]
            for j in range(1, per_tile + 1):
                mine += own_placed[j][k : k + 1, :] * gradient[:, j * box : (j + 1) * box]
            weighted = seds[k : k + 1, :] * mine
            if band == 0:
                terms[at, :box, :] = weighted
                terms[at, box:, :] = jnp.zeros((terms.shape[1] - box, box), F32)
            else:
                terms[at, :box, :] += weighted
            terms[at, box + band : box + band + 1, :] = jnp.sum(
                mine * parts[1][4](k), axis=0, keepdims=True
            )
    for store in stores:
        store.wait()


def last_kernel(count, *refs):
    received, (morph, sed, gamma, new_morph, new_sed) = refs[:count], refs[count:]
    box = morph.shape[1]
    bands = sed.shape[1]
    for k in range(morph.shape[0]):
        total = received[0][k]
        for ref in received[1:]:
            total += ref[k]
        mine = morph[k]
        spectrum = sed[k : k + 1, :]
        step = gamma[k : k + 1, :]
        step_morph = step / jnp.sum(spectrum * spectrum, axis=1, keepdims=True)
        new_morph[k] = jnp.maximum(mine + step_morph * total[:box], 0.0)
        squares = jnp.sum(jnp.sum(mine * mine, axis=0, keepdims=True), axis=1, keepdims=True)
        step_sed = step / jnp.sqrt(squares)
        sums = jnp.sum(total[box : box + bands], axis=1, keepdims=True)
        eye = lax.broadcasted_iota(jnp.int32, (bands, bands), 0) == lax.broadcasted_iota(
            jnp.int32, (bands, bands), 1
        )
        sed_grad = jnp.sum(jnp.where(eye, sums, 0.0), axis=0, keepdims=True)
        new_sed[k : k + 1, :] = jnp.maximum(spectrum + step_sed * sed_grad, 0.0)


def body(observed, inverse_variance, sed, morph, foot_block, gamma, row_kernel, col_kernel):
    bands, rows, cols = observed.shape
    sources, box = morph.shape[1:3]
    reach = (row_kernel.shape[1] - 1) // 2
    halo, rim = up_to(reach, 8), up_to(2 * reach, 8)
    extra = up_to(bands, 8)
    shape = (rows, cols, box, reach, halo, rim)
    tiles, tile_rows = lax.axis_size("tx"), lax.axis_size("ty")
    chips = tiles // 2
    paired = chips & (chips - 1) == 0

    def hop(value, distance, back=False):
        if paired:
            pairs = [(i, i ^ (2 * distance)) for i in range(tiles)]
        else:
            pairs = [(i, (i + 2 * distance) % tiles) for i in range(tiles)]
            pairs = [(j, i) for i, j in pairs] if back else pairs
        return lax.ppermute(value, "tx", pairs)

    def swap(value):
        return lax.ppermute(value, "tx", [(i, i ^ 1) for i in range(tiles)])

    info = jnp.concatenate([sed[0], foot_block[0][:, None].astype(F32)], axis=1)
    info = jnp.pad(info[:, None, :], ((0, 0), (0, extra - 1), (0, box - bands - 1)))
    block = jnp.concatenate([morph[0], info], axis=1)
    same = jnp.concatenate([block] + [hop(block, d) for d in range(1, chips)], axis=0)
    other = swap(same)

    up = [(i, i + 1) for i in range(tile_rows - 1)]
    down = [(j, i) for i, j in up]
    bottom = jnp.concatenate([jnp.concatenate([v[:, box - rim : box], v[:, box:]], 1) for v in (same, other)])
    top = jnp.concatenate([jnp.concatenate([v[:, :rim], v[:, box:]], 1) for v in (same, other)])
    above = lax.ppermute(bottom, "ty", up)
    below = lax.ppermute(top, "ty", down)
    images = jnp.concatenate([observed, inverse_variance])
    halo_above = lax.ppermute(images[:, rows - halo :], "ty", up)
    halo_below = lax.ppermute(images[:, :halo], "ty", down)

    matrices = band_matrices(row_kernel, col_kernel, shape)
    row = lax.axis_index("ty")
    place = jnp.stack([lax.axis_index("tx") * (cols // box), row, tile_rows - 1 - row]).astype(jnp.int32)
    terms = jax.ShapeDtypeStruct((chips * sources, box + extra, box), F32)
    residual, terms_same, terms_other = pl.pallas_call(
        functools.partial(main_kernel, shape),
        out_shape=[jax.ShapeDtypeStruct(observed.shape, F32), terms, terms],
        in_specs=[SMEM] + [VMEM] * 6 + [HBM] * 2 + [VMEM] * 6,
        out_specs=[HBM, VMEM, VMEM],
        scratch_shapes=[pltpu.VMEM(observed.shape, F32)] * 3
        + [
            pltpu.VMEM((rows + 2 * rim, cols + box), F32),
            pltpu.SemaphoreType.DMA((3, bands)),
        ],
        compiler_params=pltpu.CompilerParams(vmem_limit_bytes=LIMIT),
        name="deblend_step",
    )(place, same, other, above, below, halo_above, halo_below, observed, inverse_variance, *matrices)

    chip_terms = terms_same + swap(terms_other)
    per_chip = chip_terms.reshape(chips, sources, box + extra, box)
    received = [per_chip[0]] + [hop(per_chip[d], d, back=True) for d in range(1, chips)]
    new_morph, new_sed = pl.pallas_call(
        functools.partial(last_kernel, len(received)),
        out_shape=[
            jax.ShapeDtypeStruct(morph.shape[1:], F32),
            jax.ShapeDtypeStruct(sed.shape[1:], F32),
        ],
        in_specs=[VMEM] * (len(received) + 3),
        out_specs=[VMEM] * 2,
        compiler_params=pltpu.CompilerParams(vmem_limit_bytes=LIMIT),
        name="update",
    )(*received, morph[0], sed[0], gamma[0][:, None])
    return residual, new_morph[None], new_sed[None]


def solution(mesh):
    tile = P(None, "ty", "tx")
    source = P("ty", "tx")
    return jax.shard_map(
        body,
        mesh=mesh,
        in_specs=(tile, tile, source, source, source, source, P(), P()),
        out_specs=(tile, source, source),
        check_vma=False,
    )
```

```python
import functools

import jax
import jax.numpy as jnp
from jax import lax
from jax.experimental import pallas as pl
from jax.experimental.pallas import tpu as pltpu
from jax.sharding import PartitionSpec as P

F32 = jnp.float32
BF16 = jnp.bfloat16
VMEM = pl.BlockSpec(memory_space=pltpu.VMEM)
SMEM = pl.BlockSpec(memory_space=pltpu.SMEM)
HBM = pl.BlockSpec(memory_space=pltpu.HBM)
MIB = 1024 * 1024


def params(mebibytes):
    return pltpu.CompilerParams(vmem_limit_bytes=mebibytes * MIB)


def up_to(value, step):
    return -(-value // step) * step


def halves(value):
    high = value.astype(BF16)
    return high, (value - high.astype(F32)).astype(BF16)


def product(left, right):
    dot = functools.partial(jnp.dot, preferred_element_type=F32)
    (lh, ll), (rh, rl) = left, right
    return dot(lh, rh) + (dot(lh, rl) + dot(ll, rh))


class Sizes:
    def __init__(self, observed, morph, taps):
        self.bands, self.rows, self.cols = observed
        self.box = morph[-1]
        self.per_tile = self.cols // self.box
        self.taps = taps
        self.reach = (taps - 1) // 2
        self.halo = up_to(self.reach, 8)
        self.rim = up_to(2 * self.reach, 8)
        self.tall = self.rows + 2 * self.halo
        self.near = self.halo + up_to(self.reach, 8)
        self.extra = up_to(self.bands, 8)


def prepare_kernel(z, row_ref, flip_row_ref, col_ref, flip_col_ref, observed, weights, *out):
    mats, (observed_out, weights_out, sems) = out[:12], out[12:]
    cols_m, grad_m, tall_m, above_m, below_m, back_m = [mats[i : i + 2] for i in range(0, 12, 2)]
    copies = [
        pltpu.make_async_copy(observed, observed_out, sems.at[0]),
        pltpu.make_async_copy(weights, weights_out, sems.at[1]),
    ]
    for copy in copies:
        copy.start()

    box = z.box

    def cycle(ref, band, count, shift):
        row = pltpu.roll(jnp.broadcast_to(ref[band : band + 1, :], (8, box)), shift % box, 1)
        spread = jnp.broadcast_to(row[:1, :], (count, box))
        return pltpu.roll(spread, 0, 1, stride=1, stride_axis=0)

    def tap(count, start, shift):
        at = lax.broadcasted_iota(jnp.int32, (count, box), 1)
        at += start - shift - lax.broadcasted_iota(jnp.int32, (count, box), 0)
        return (at >= 0) & (at < z.taps)

    def cut(value, mask):
        return halves(jnp.where(mask, value, 0.0))

    def keep(pair, band, value, rows=slice(None), lanes=slice(None)):
        for ref, half in zip(pair, value):
            ref[band, rows, lanes] = half

    lower = lax.broadcasted_iota(jnp.int32, (box, box), 0) >= box // 2
    right = lax.broadcasted_iota(jnp.int32, (box, box), 1) >= box // 2
    none = [jnp.zeros((box, box), BF16)] * 2
    whole = [slice(i * box, (i + 1) * box) for i in range(z.per_tile + 1)]
    col_shift = -z.reach
    tall_shift = -z.halo - z.reach
    above_shift = z.rim - z.halo - z.reach
    below_shift = z.tall - z.near - z.halo - z.rows - z.reach
    back_shift = z.halo - z.reach
    apart = {d: tap(box, d * box, col_shift) for d in (-1, 0, 1)}
    tall_mask = tap(z.tall, 0, tall_shift)
    above_mask = tap(z.near, 0, above_shift)
    below_mask = tap(z.near, 0, below_shift)
    back_masks = [tap(z.rows, start, back_shift) for start in range(0, z.tall, box)]
    for band in range(z.bands):
        strip = cycle(col_ref, band, box, col_shift)
        block = {d: cut(strip, apart[d]) for d in apart}
        turned = cycle(flip_col_ref, band, box, col_shift)
        flipped = {d: cut(turned, apart[d]) for d in apart}
        for i in range(z.per_tile):
            for j in range(z.per_tile):
                keep(cols_m, band, block.get(j - i, none), whole[i], whole[j])
                keep(grad_m, band, flipped.get(j - i, none), whole[i], whole[j])
        for i in range(z.per_tile):
            before = block[1] if i == 0 else none
            after = block[-1] if i == z.per_tile - 1 else none
            edge = [jnp.where(lower, p, q) for p, q in zip(before, after)]
            keep(cols_m, band, edge, whole[z.per_tile], whole[i])
            before = flipped[-1] if i == 0 else none
            after = flipped[1] if i == z.per_tile - 1 else none
            edge = [jnp.where(right, p, q) for p, q in zip(before, after)]
            keep(grad_m, band, edge, whole[i], whole[z.per_tile])
        keep(tall_m, band, cut(cycle(flip_row_ref, band, z.tall, tall_shift), tall_mask))
        for pair, shift, mask in (
            (above_m, above_shift, above_mask),
            (below_m, below_shift, below_mask),
        ):
            value = cut(cycle(flip_row_ref, band, z.near, shift), mask)
            keep(pair, band, [h[:, : z.rim] for h in value])
        value = cycle(row_ref, band, z.rows, back_shift)
        for index, mask in enumerate(back_masks):
            start = index * box
            size = min(box, z.tall - start)
            part = [h[:, :size] for h in cut(value, mask)]
            keep(back_m, band, part, lanes=slice(start, start + size))
    for copy in copies:
        copy.wait()


def prepare(row_kernel, col_kernel, observed, weights, z):
    pad = lambda kernel: jnp.pad(kernel, ((0, 0), (0, z.box - z.taps)))
    sizes = [
        (z.cols + z.box, z.cols),
        (z.cols, z.cols + z.box),
        (z.tall, z.rows),
        (z.near, z.rim),
        (z.near, z.rim),
        (z.rows, z.tall),
    ]
    flat = pl.pallas_call(
        functools.partial(prepare_kernel, z),
        out_shape=[jax.ShapeDtypeStruct((z.bands,) + s, BF16) for s in sizes for _ in range(2)]
        + [jax.ShapeDtypeStruct(observed.shape, F32)] * 2,
        in_specs=[VMEM] * 4 + [HBM] * 2,
        out_specs=[VMEM] * 14,
        scratch_shapes=[pltpu.SemaphoreType.DMA((2,))],
        compiler_params=params(8),
        cost_estimate=pl.CostEstimate(flops=10**9, bytes_accessed=10**7, transcendentals=0),
        name="prepare",
    )(
        pad(row_kernel), pad(row_kernel[:, ::-1]), pad(col_kernel), pad(col_kernel[:, ::-1]),
        observed, weights,
    )
    return [flat[i : i + 2] for i in range(0, 12, 2)], flat[12:]


def box_of(z, foot, first):
    place = foot.astype(jnp.int32) - first
    inside = (place >= 0) & (place < z.per_tile)
    near = (place >= -1) & (place <= z.per_tile)
    box = jnp.where(inside, place, z.per_tile)
    low = jnp.where(place == -1, z.box // 2, 0)
    high = jnp.where(place == z.per_tile, z.box // 2, z.box)
    return near, pl.ds(pl.multiple_of(box * z.box, z.box), z.box), low, high


def add_sources(z, place, valid, info, offset, source, count, model, start, length):
    lane = lax.broadcasted_iota(jnp.int32, (length, z.box), 1)

    def step(k, _):
        near, at, low, high = box_of(z, info[offset + k, z.bands], place[0])

        @pl.when(near & valid)
        def _():
            value = jnp.where((lane >= low) & (lane < high), source[k, :length, :], 0.0)
            for band in range(z.bands):
                model[band, start : start + length, at] += info[offset + k, band] * value

        return 0

    lax.fori_loop(0, count, step, 0)


def inner_kernel(z, place, info, same, other, *refs):
    cols_h, cols_l, tall_h, tall_l, predicted, model = refs
    half = same.shape[0]
    model[...] = jnp.zeros(model.shape, F32)
    add_sources(z, place, True, info, 0, same, half, model, 0, z.rows)
    add_sources(z, place, True, info, half, other, half, model, 0, z.rows)
    for band in range(z.bands):
        blurred = product(halves(model[band]), (cols_h[band], cols_l[band]))
        predicted[band] = product((tall_h[band], tall_l[band]), halves(blurred))


def outer_kernel(z, place, info, info_far, same, other, far, images_0, images_1, *refs):
    observed, weights, predicted = refs[:3]
    cols_m, grad_m, above_m, below_m, back_m = [refs[i : i + 2] for i in range(3, 13, 2)]
    residual_hbm, terms_same, terms_other = refs[13:16]
    residual, model, gradient, sems = refs[16:]
    half = same.shape[0]
    model[...] = jnp.zeros(model.shape, F32)
    count = 2 * half
    odd = place[3]
    for valid, which, start in ((place[1] > 0, 1 - odd, 0), (place[2] > 0, odd, z.rim)):
        source = far.at[which]
        add_sources(z, place, valid, info_far, which * count, source, count, model, start, z.rim)
    stores = []
    rest = z.tall - z.near
    middle = slice(z.halo, z.halo + z.rows)
    for band in range(z.bands):
        blurred = product(halves(model[band]), (cols_m[0][band], cols_m[1][band]))
        first = product((above_m[0][band], above_m[1][band]), halves(blurred[: z.rim]))
        last = product((below_m[0][band], below_m[1][band]), halves(blurred[z.rim :]))
        whole = jnp.concatenate(
            [
                predicted[band, : z.near] + first,
                predicted[band, z.near : rest],
                predicted[band, rest:] + last,
            ],
            0,
        )
        residual[band, middle] = weights[band] * (observed[band] - whole[middle])
        store = pltpu.make_async_copy(
            residual.at[band, middle], residual_hbm.at[band], sems.at[band]
        )
        store.start()
        stores.append(store)
        images = [
            [ref[part + band] for ref in (images_0, images_1)] for part in (0, z.bands)
        ]
        seen, weight = [jnp.where(odd > 0, a, b) for a, b in images]
        residual[band, : z.halo] = weight * (seen - whole[: z.halo])
        seen, weight = [jnp.where(odd > 0, b, a) for a, b in images]
        residual[band, z.halo + z.rows :] = weight * (seen - whole[z.halo + z.rows :])
    for band in range(z.bands):
        backrows = product((back_m[0][band], back_m[1][band]), halves(residual[band]))
        gradient[band] = product(halves(backrows), (grad_m[0][band], grad_m[1][band]))

    lane = lax.broadcasted_iota(jnp.int32, (z.rows, z.box), 1)
    for side, (source, terms) in enumerate(((same, terms_same), (other, terms_other))):

        def step(k, _, side=side, source=source, terms=terms):
            at_info = side * half + k
            near, at, low, high = box_of(z, info[at_info, z.bands], place[0])

            @pl.when(near)
            def _():
                keep = (lane >= low) & (lane < high)
                shape = jnp.where(keep, source[k, : z.rows, :], 0.0)
                total = jnp.zeros((z.rows, z.box), F32)
                for band in range(z.bands):
                    value = gradient[band, :, at]
                    total += info[at_info, band] * value
                    terms[k, z.box + band : z.box + band + 1, :] = jnp.sum(
                        shape * value, axis=0, keepdims=True
                    )
                terms[k, : z.box, :] = jnp.where(keep, total, 0.0)
                unused = terms.shape[1] - z.box - z.bands
                if unused:
                    terms[k, z.box + z.bands :, :] = jnp.zeros((unused, z.box), F32)

            @pl.when(jnp.logical_not(near))
            def _():
                terms[k] = jnp.zeros(terms.shape[1:], F32)

            return 0

        lax.fori_loop(0, half, step, 0)
    for store in stores:
        store.wait()


def inner_call(z, place, table, same, other, cols_m, tall_m):
    return pl.pallas_call(
        functools.partial(inner_kernel, z),
        out_shape=jax.ShapeDtypeStruct((z.bands, z.tall, z.cols), F32),
        in_specs=[SMEM] * 2 + [VMEM] * 6,
        out_specs=VMEM,
        scratch_shapes=[pltpu.VMEM((z.bands, z.rows, z.cols + z.box), F32)],
        compiler_params=params(8),
        cost_estimate=pl.CostEstimate(flops=10**9, bytes_accessed=10**7, transcendentals=0),
        name="inner_rows",
    )(place, table, same, other, *cols_m, *tall_m)


def outer_call(z, terms, place, table, far_table, same, other, far, images_0, images_1, observed,
               weights, predicted, cols_m, grad_m, above_m, below_m, back_m):
    return pl.pallas_call(
        functools.partial(outer_kernel, z),
        out_shape=[jax.ShapeDtypeStruct(observed.shape, F32), terms, terms],
        in_specs=[SMEM] * 3 + [VMEM] * 18,
        out_specs=[HBM, VMEM, VMEM],
        scratch_shapes=[
            pltpu.VMEM((z.bands, z.tall, z.cols), F32),
            pltpu.VMEM((z.bands, 2 * z.rim, z.cols + z.box), F32),
            pltpu.VMEM((z.bands, z.rows, z.cols + z.box), F32),
            pltpu.SemaphoreType.DMA((z.bands,)),
        ],
        compiler_params=params(12),
        name="whole_step",
    )(
        place, table, far_table, same, other, far, images_0, images_1, observed, weights,
        predicted, *cols_m, *grad_m, *above_m, *below_m, *back_m,
    )


def last_kernel(count, *refs):
    received, (morph, sed, gamma, new_morph, new_sed) = refs[:count], refs[count:]
    box = morph.shape[1]
    bands = sed.shape[1]
    for k in range(morph.shape[0]):
        total = received[0][k]
        for ref in received[1:]:
            total += ref[k]
        mine = morph[k]
        spectrum = sed[k : k + 1, :]
        step = gamma[k : k + 1, :]
        step_morph = step / jnp.sum(spectrum * spectrum, axis=1, keepdims=True)
        new_morph[k] = jnp.maximum(mine + step_morph * total[:box], 0.0)
        squares = jnp.sum(jnp.sum(mine * mine, axis=0, keepdims=True), axis=1, keepdims=True)
        step_sed = step / jnp.sqrt(squares)
        sums = jnp.sum(total[box : box + bands], axis=1, keepdims=True)
        eye = lax.broadcasted_iota(jnp.int32, (bands, bands), 0) == lax.broadcasted_iota(
            jnp.int32, (bands, bands), 1
        )
        sed_grad = jnp.sum(jnp.where(eye, sums, 0.0), axis=0, keepdims=True)
        new_sed[k : k + 1, :] = jnp.maximum(spectrum + step_sed * sed_grad, 0.0)


def body(observed, inverse_variance, sed, morph, foot_block, gamma, row_kernel, col_kernel):
    z = Sizes(observed.shape, morph.shape, row_kernel.shape[1])
    sources = morph.shape[1]
    tiles, tile_rows = lax.axis_size("tx"), lax.axis_size("ty")
    chips = tiles // 2
    paired = chips & (chips - 1) == 0

    def hop(value, distance, back=False):
        if paired:
            pairs = [(i, i ^ (2 * distance)) for i in range(tiles)]
        else:
            pairs = [(i, (i + 2 * distance) % tiles) for i in range(tiles)]
            pairs = [(j, i) for i, j in pairs] if back else pairs
        return lax.ppermute(value, "tx", pairs)

    def swap(value):
        return lax.ppermute(value, "tx", [(i, i ^ 1) for i in range(tiles)])

    below = z.extra - 1
    block = (
        jnp.pad(morph[0], ((0, 0), (0, z.extra), (0, 0)))
        + jnp.pad(sed[0][:, None], ((0, 0), (z.box, below), (0, z.box - z.bands)))
        + jnp.pad(
            foot_block[0][:, None, None].astype(F32),
            ((0, 0), (z.box, below), (z.bands, z.box - z.bands - 1)),
        )
    )
    same = jnp.concatenate([block] + [hop(block, d) for d in range(1, chips)], axis=0)
    other = swap(same)

    row = lax.axis_index("ty")
    odd = row % 2

    def exchange(values, length, last=None):
        received = []
        for start in (0, 1):
            pairs = [(i, i + 1) for i in range(start, tile_rows - 1, 2)]
            edge = jnp.where(odd == start, z.rows - length, 0)
            parts = [lax.dynamic_slice_in_dim(v, edge, length, axis=1) for v in values]
            sent = jnp.concatenate(parts) if last is None else jnp.concatenate(parts + [last], axis=1)
            values, sent = lax.optimization_barrier((values, sent))
            received.append(lax.ppermute(sent, "ty", pairs + [(j, i) for i, j in pairs]))
        return received

    images = exchange((observed, inverse_variance), z.halo)
    strips = exchange((same[:, : z.box],), z.rim, same[:, z.box :])
    far_same = jnp.stack(strips)
    far = jnp.concatenate([far_same, swap(far_same)], axis=1)

    matrices, (observed_near, weights_near) = prepare(
        row_kernel, col_kernel, observed, inverse_variance, z
    )
    cols_m, grad_m, tall_m, above_m, below_m, back_m = matrices
    first = lax.axis_index("tx") * z.per_tile
    place = jnp.stack([first, row, tile_rows - 1 - row, odd]).astype(jnp.int32)
    table = jnp.concatenate([same[:, z.box], other[:, z.box]])[:, : z.bands + 1]
    far_table = far[:, :, z.rim, : z.bands + 1].reshape(-1, z.bands + 1)
    predicted = inner_call(z, place, table, same, other, cols_m, tall_m)
    terms = jax.ShapeDtypeStruct((chips * sources, z.box + z.extra, z.box), F32)
    residual, terms_same, terms_other = outer_call(
        z, terms, place, table, far_table, same, other, far, *images, observed_near, weights_near,
        predicted, cols_m, grad_m, above_m, below_m, back_m,
    )

    chip_terms = terms_same + swap(terms_other)
    per_chip = chip_terms.reshape(chips, sources, z.box + z.extra, z.box)
    received = [per_chip[0]] + [hop(per_chip[d], d, back=True) for d in range(1, chips)]
    new_morph, new_sed = pl.pallas_call(
        functools.partial(last_kernel, len(received)),
        out_shape=[
            jax.ShapeDtypeStruct(morph.shape[1:], F32),
            jax.ShapeDtypeStruct(sed.shape[1:], F32),
        ],
        in_specs=[VMEM] * (len(received) + 3),
        out_specs=[VMEM] * 2,
        compiler_params=params(8),
        name="update",
    )(*received, morph[0], sed[0], gamma[0][:, None])
    return residual, new_morph[None], new_sed[None]


def solution(mesh):
    tile = P(None, "ty", "tx")
    source = P("ty", "tx")
    return jax.shard_map(
        body,
        mesh=mesh,
        in_specs=(tile, tile, source, source, source, source, P(), P()),
        out_specs=(tile, source, source),
        check_vma=False,
    )
```

```python
import functools

import jax
import jax.numpy as jnp
from jax import lax
from jax.experimental import pallas as pl
from jax.experimental.pallas import tpu as pltpu
from jax.sharding import PartitionSpec as P

F32 = jnp.float32
BF16 = jnp.bfloat16
VMEM = pl.BlockSpec(memory_space=pltpu.VMEM)
SMEM = pl.BlockSpec(memory_space=pltpu.SMEM)
HBM = pl.BlockSpec(memory_space=pltpu.HBM)
MIB = 1024 * 1024


def params(mebibytes):
    return pltpu.CompilerParams(vmem_limit_bytes=mebibytes * MIB)


def up_to(value, step):
    return -(-value // step) * step


def halves(value):
    high = value.astype(BF16)
    return high, (value - high.astype(F32)).astype(BF16)


def product(left, right):
    dot = functools.partial(jnp.dot, preferred_element_type=F32)
    (lh, ll), (rh, rl) = left, right
    rows = lh.shape[0]
    both = dot(jnp.concatenate([lh, ll], 0), rh)
    return both[:rows] + (dot(lh, rl) + both[rows:])


class Sizes:
    def __init__(self, observed, morph, taps):
        self.bands, self.rows, self.cols = observed
        self.box = morph[-1]
        self.per_tile = self.cols // self.box
        self.taps = taps
        self.reach = (taps - 1) // 2
        self.halo = up_to(self.reach, 8)
        self.rim = up_to(2 * self.reach, 8)
        self.tall = self.rows + 2 * self.halo
        self.near = self.halo + up_to(self.reach, 8)
        self.extra = up_to(self.bands, 8)


def prepare_kernel(z, place, row_ref, col_ref, observed, weights, *out):
    mats, out = out[2:14], out[14:]
    observed_out, weights_out, done, row_taps, col_taps, cycles, turned, sems = out
    cols_m, grad_m, tall_m, above_m, below_m, back_m = [mats[i : i + 2] for i in range(0, 12, 2)]
    copies = [
        pltpu.make_async_copy(observed, observed_out, sems.at[0]),
        pltpu.make_async_copy(weights, weights_out, sems.at[1]),
    ]
    for copy in copies:
        copy.start()

    box = z.box

    row_taps[...] = jnp.zeros(row_taps.shape, F32)
    col_taps[...] = jnp.zeros(col_taps.shape, F32)
    row_taps[: z.bands, : z.taps] = row_ref[...]
    col_taps[: z.bands, : z.taps] = col_ref[...]

    def cycle(ref, band, shift):
        row = pltpu.roll(jnp.broadcast_to(ref[band : band + 1, :], (8, box)), shift % box, 1)
        spread = jnp.broadcast_to(row[:1, :], (box, box))
        return pltpu.roll(spread, 0, 1, stride=1, stride_axis=0)

    def turn(value, count, shift):
        value = pltpu.roll(value, shift % box, 1)
        return jnp.concatenate([value, value], 0)[:count]

    def tap(count, start, shift):
        at = lax.broadcasted_iota(jnp.int32, (count, box), 1)
        at += start - shift - lax.broadcasted_iota(jnp.int32, (count, box), 0)
        return ((at >= 0) & (at < z.taps)).astype(F32).astype(BF16)

    def cut(value, mask):
        return [half * mask for half in halves(value)]

    def keep(pair, band, value, rows=slice(None), lanes=slice(None)):
        for ref, half in zip(pair, value):
            ref[band, rows, lanes] = half

    as_half = lambda mask: mask.astype(F32).astype(BF16)
    at_row = lax.broadcasted_iota(jnp.int32, (box, box), 0)
    at_lane = lax.broadcasted_iota(jnp.int32, (box, box), 1)
    lower, upper = as_half(at_row >= box // 2), as_half(at_row < box // 2)
    right, left = as_half(at_lane >= box // 2), as_half(at_lane < box // 2)
    none = [jnp.zeros((box, box), BF16)] * 2
    whole = [slice(i * box, (i + 1) * box) for i in range(z.per_tile + 1)]
    col_shift = -z.reach
    tall_shift = -z.halo - z.reach
    above_shift = z.rim - z.halo - z.reach
    below_shift = z.tall - z.near - z.halo - z.rows - z.reach
    back_shift = z.halo - z.reach
    flip_shift = lambda shift: shift + 2 * z.reach + back_shift
    apart = {d: tap(box, d * box, col_shift) for d in (-1, 0, 1)}
    tall_mask = tap(z.tall, 0, tall_shift)
    above_mask = tap(z.near, 0, above_shift)
    below_mask = tap(z.near, 0, below_shift)
    back_masks = [tap(z.rows, start, back_shift) for start in range(0, z.tall, box)]
    for band in range(z.bands):
        cycles[band] = cycle(col_taps, band, col_shift)
        cycles[z.bands + band] = cycle(row_taps, band, back_shift)
    for index in range(2 * z.bands):
        turned[index] = cycles[index].T
    for band in range(z.bands):
        block = {d: cut(cycles[band], apart[d]) for d in apart}
        flipped = {d: cut(turned[band], apart[d]) for d in apart}
        for i in range(z.per_tile):
            for j in range(z.per_tile):
                keep(cols_m, band, block.get(j - i, none), whole[i], whole[j])
                keep(grad_m, band, flipped.get(j - i, none), whole[i], whole[j])
        for i in range(z.per_tile):
            edge = none
            if i == 0:
                edge = [p + h * lower for p, h in zip(edge, block[1])]
            if i == z.per_tile - 1:
                edge = [p + h * upper for p, h in zip(edge, block[-1])]
            keep(cols_m, band, edge, whole[z.per_tile], whole[i])
            edge = none
            if i == 0:
                edge = [p + h * right for p, h in zip(edge, flipped[-1])]
            if i == z.per_tile - 1:
                edge = [p + h * left for p, h in zip(edge, flipped[1])]
            keep(grad_m, band, edge, whole[i], whole[z.per_tile])
    for band in range(z.bands):
        value, flip = cycles[z.bands + band], turned[z.bands + band]
        keep(tall_m, band, cut(turn(flip, z.tall, flip_shift(tall_shift)), tall_mask))
        for pair, shift, mask in (
            (above_m, above_shift, above_mask),
            (below_m, below_shift, below_mask),
        ):
            part = cut(turn(flip, z.near, flip_shift(shift)), mask)
            keep(pair, band, [h[:, : z.rim] for h in part])
        for index, mask in enumerate(back_masks):
            start = index * box
            size = min(box, z.tall - start)
            part = [h[:, :size] for h in cut(value, mask)]
            keep(back_m, band, part, lanes=slice(start, start + size))
    for copy in copies:
        copy.wait()
    done[...] = jnp.zeros(done.shape, F32)


def prepare(z, place, row_kernel, col_kernel, observed, weights, images):
    sizes = [
        (z.cols + z.box, z.cols),
        (z.cols, z.cols + z.box),
        (z.tall, z.rows),
        (z.near, z.rim),
        (z.near, z.rim),
        (z.rows, z.tall),
    ]
    return pl.pallas_call(
        functools.partial(prepare_kernel, z),
        out_shape=[jax.ShapeDtypeStruct((z.bands,) + s, BF16) for s in sizes for _ in range(2)]
        + [jax.ShapeDtypeStruct(observed.shape, F32)] * 2
        + [jax.ShapeDtypeStruct((8, 128), F32)],
        in_specs=[SMEM] + [VMEM] * 2 + [HBM] * 4,
        out_specs=[VMEM] * 15,
        scratch_shapes=[pltpu.VMEM((up_to(z.bands, 8), z.box), F32)] * 2
        + [pltpu.VMEM((2 * z.bands, z.box, z.box), F32)] * 2
        + [pltpu.SemaphoreType.DMA((2,))],
        compiler_params=params(8),
        cost_estimate=pl.CostEstimate(flops=10**9, bytes_accessed=10**7, transcendentals=0),
        name="prepare",
    )(place, row_kernel, col_kernel, observed, weights, *images)


def box_of(z, foot, first):
    place = foot.astype(jnp.int32) - first
    inside = (place >= 0) & (place < z.per_tile)
    near = (place >= -1) & (place <= z.per_tile)
    box = jnp.where(inside, place, z.per_tile)
    low = jnp.where(place == -1, z.box // 2, 0)
    high = jnp.where(place == z.per_tile, z.box // 2, z.box)
    return near, pl.ds(pl.multiple_of(box * z.box, z.box), z.box), low, high


def add_sources(z, place, valid, info, offset, source, count, row, model, start, length):
    lane = lax.broadcasted_iota(jnp.int32, (length, z.box), 1)

    def step(k, _):
        near, at, low, high = box_of(z, info[offset + k, z.bands], place[0])

        @pl.when(near)
        def _():
            value = jnp.where((lane >= low) & (lane < high), source[k, row : row + length, :], 0.0)
            for band in range(z.bands):
                model[band, start : start + length, at] += info[offset + k, band] * value

        return 0

    @pl.when(valid)
    def _():
        lax.fori_loop(0, count, step, 0)


def inner_kernel(z, place, info, done, same, other, *refs):
    cols_h, cols_l, tall_h, tall_l, predicted, model, blurred = refs
    half = same.shape[0]
    model[...] = jnp.zeros(model.shape, F32)
    add_sources(z, place, place[3] >= 0, info, 0, same, half, z.extra, model, 0, z.rows)
    add_sources(z, place, place[3] >= 0, info, half, other, half, z.extra, model, 0, z.rows)
    for band in range(z.bands):
        blurred[band] = product(halves(model[band]), (cols_h[band], cols_l[band]))
    for band in range(z.bands):
        predicted[band] = product((tall_h[band], tall_l[band]), halves(blurred[band]))


def outer_kernel(z, place, info, info_far, same, other, far_0, far_1, images_0, images_1, *refs):
    observed, weights, predicted = refs[:3]
    cols_m, grad_m, above_m, below_m, back_m = [refs[i : i + 2] for i in range(3, 13, 2)]
    residual_hbm, terms_same, terms_other = refs[13:16]
    residual, model, gradient, backrows, blurred, sems = refs[16:]
    half = same.shape[0]
    model[...] = jnp.zeros(model.shape, F32)
    count = 2 * half
    odd = place[3]
    for which, far in enumerate((far_0, far_1)):
        above = (odd != which) & (place[1] > 0)
        below = (odd == which) & (place[2] > 0)
        first, last = (2 + which) * count, which * count
        add_sources(z, place, above, info_far, first, far, count, 0, model, 0, z.rim)
        add_sources(z, place, below, info_far, last, far, count, z.extra, model, z.rim, z.rim)
    stores = []
    rest = z.tall - z.near
    middle = slice(z.halo, z.halo + z.rows)
    for band in range(z.bands):
        blurred[band] = product(halves(model[band]), (cols_m[0][band], cols_m[1][band]))
    for band in range(z.bands):
        first = product((above_m[0][band], above_m[1][band]), halves(blurred[band, : z.rim]))
        last = product((below_m[0][band], below_m[1][band]), halves(blurred[band, z.rim :]))
        whole = jnp.concatenate(
            [
                predicted[band, : z.near] + first,
                predicted[band, z.near : rest],
                predicted[band, rest:] + last,
            ],
            0,
        )
        residual[band, middle] = weights[band] * (observed[band] - whole[middle])
        store = pltpu.make_async_copy(
            residual.at[band, middle], residual_hbm.at[band], sems.at[band]
        )
        store.start()
        stores.append(store)
        images = [
            [ref[part + band] for ref in (images_0, images_1)] for part in (0, z.bands)
        ]
        seen, weight = [jnp.where(odd > 0, a, b) for a, b in images]
        residual[band, : z.halo] = weight * (seen - whole[: z.halo])
        seen, weight = [jnp.where(odd > 0, b, a) for a, b in images]
        residual[band, z.halo + z.rows :] = weight * (seen - whole[z.halo + z.rows :])
    for band in range(z.bands):
        backrows[band] = product((back_m[0][band], back_m[1][band]), halves(residual[band]))
    for band in range(z.bands):
        gradient[band] = product(halves(backrows[band]), (grad_m[0][band], grad_m[1][band]))

    lane = lax.broadcasted_iota(jnp.int32, (z.rows, z.box), 1)
    for side, (source, terms) in enumerate(((same, terms_same), (other, terms_other))):

        def step(k, _, side=side, source=source, terms=terms):
            at_info = side * half + k
            near, at, low, high = box_of(z, info[at_info, z.bands], place[0])

            @pl.when(near)
            def _():
                keep = (lane >= low) & (lane < high)
                shape = jnp.where(keep, source[k, z.extra : z.extra + z.rows, :], 0.0)
                total = jnp.zeros((z.rows, z.box), F32)
                for band in range(z.bands):
                    value = gradient[band, :, at]
                    total += info[at_info, band] * value
                    terms[k, z.box + band : z.box + band + 1, :] = jnp.sum(
                        shape * value, axis=0, keepdims=True
                    )
                terms[k, : z.box, :] = jnp.where(keep, total, 0.0)
                unused = terms.shape[1] - z.box - z.bands
                if unused:
                    terms[k, z.box + z.bands :, :] = jnp.zeros((unused, z.box), F32)

            @pl.when(jnp.logical_not(near))
            def _():
                terms[k] = jnp.zeros(terms.shape[1:], F32)

            return 0

        lax.fori_loop(0, half, step, 0)
    for store in stores:
        store.wait()


def inner_call(z, place, table, done, same, other, cols_m, tall_m):
    return pl.pallas_call(
        functools.partial(inner_kernel, z),
        out_shape=jax.ShapeDtypeStruct((z.bands, z.tall, z.cols), F32),
        in_specs=[SMEM] * 2 + [VMEM] * 7,
        out_specs=VMEM,
        scratch_shapes=[
            pltpu.VMEM((z.bands, z.rows, z.cols + z.box), F32),
            pltpu.VMEM((z.bands, z.rows, z.cols), F32),
        ],
        compiler_params=params(8),
        cost_estimate=pl.CostEstimate(flops=10**9, bytes_accessed=10**7, transcendentals=0),
        name="inner_rows",
    )(place, table, done, same, other, *cols_m, *tall_m)


def outer_call(z, terms, place, table, far_table, same, other, far_0, far_1, images_0, images_1, observed,
               weights, predicted, cols_m, grad_m, above_m, below_m, back_m):
    return pl.pallas_call(
        functools.partial(outer_kernel, z),
        out_shape=[jax.ShapeDtypeStruct(observed.shape, F32), terms, terms],
        in_specs=[SMEM] * 3 + [VMEM] * 19,
        out_specs=[HBM, VMEM, VMEM],
        scratch_shapes=[
            pltpu.VMEM((z.bands, z.tall, z.cols), F32),
            pltpu.VMEM((z.bands, 2 * z.rim, z.cols + z.box), F32),
            pltpu.VMEM((z.bands, z.rows, z.cols + z.box), F32),
            pltpu.VMEM((z.bands, z.rows, z.cols), F32),
            pltpu.VMEM((z.bands, 2 * z.rim, z.cols), F32),
            pltpu.SemaphoreType.DMA((z.bands,)),
        ],
        compiler_params=params(12),
        name="whole_step",
    )(
        place, table, far_table, same, other, far_0, far_1, images_0, images_1, observed, weights,
        predicted, *cols_m, *grad_m, *above_m, *below_m, *back_m,
    )


def last_kernel(count, *refs):
    received, (morph, sed, gamma, new_morph, new_sed) = refs[:count], refs[count:]
    box = morph.shape[1]
    bands = sed.shape[1]
    for k in range(morph.shape[0]):
        total = received[0][k]
        for ref in received[1:]:
            total += ref[k]
        mine = morph[k]
        spectrum = sed[k : k + 1, :]
        step = gamma[k : k + 1, :]
        step_morph = step / jnp.sum(spectrum * spectrum, axis=1, keepdims=True)
        new_morph[k] = jnp.maximum(mine + step_morph * total[:box], 0.0)
        squares = jnp.sum(jnp.sum(mine * mine, axis=0, keepdims=True), axis=1, keepdims=True)
        step_sed = step / jnp.sqrt(squares)
        sums = jnp.sum(total[box : box + bands], axis=1, keepdims=True)
        eye = lax.broadcasted_iota(jnp.int32, (bands, bands), 0) == lax.broadcasted_iota(
            jnp.int32, (bands, bands), 1
        )
        sed_grad = jnp.sum(jnp.where(eye, sums, 0.0), axis=0, keepdims=True)
        new_sed[k : k + 1, :] = jnp.maximum(spectrum + step_sed * sed_grad, 0.0)


def body(observed, inverse_variance, sed, morph, foot_block, gamma, row_kernel, col_kernel):
    z = Sizes(observed.shape, morph.shape, row_kernel.shape[1])
    sources = morph.shape[1]
    tiles, tile_rows = lax.axis_size("tx"), lax.axis_size("ty")
    chips = tiles // 2
    paired = chips & (chips - 1) == 0

    def hop(value, distance, back=False):
        if paired:
            pairs = [(i, i ^ (2 * distance)) for i in range(tiles)]
        else:
            pairs = [(i, (i + 2 * distance) % tiles) for i in range(tiles)]
            pairs = [(j, i) for i, j in pairs] if back else pairs
        return lax.ppermute(value, "tx", pairs)

    def swap(value):
        return lax.ppermute(value, "tx", [(i, i ^ 1) for i in range(tiles)])

    ends = ((0, 0), (z.extra, z.extra), (0, 0))
    block = jnp.pad(morph[0], ends)
    for start in (0, z.extra + z.box):
        rows = (start, 2 * z.extra + z.box - 1 - start)
        foot = foot_block[0][:, None, None].astype(F32)
        block += jnp.pad(sed[0][:, None], ((0, 0), rows, (0, z.box - z.bands)))
        block += jnp.pad(foot, ((0, 0), rows, (z.bands, z.box - z.bands - 1)))
    row = lax.axis_index("ty")
    odd = row % 2

    pairings = [[(i, i + 1) for i in range(start, tile_rows - 1, 2)] for start in (0, 1)]
    pairings = [pairs + [(j, i) for i, j in pairs] for pairs in pairings]
    edges = [jnp.where(odd == start, 1, 0).astype(jnp.int32) for start in (0, 1)]
    first = lax.axis_index("tx") * z.per_tile
    place = jnp.stack([first, row, tile_rows - 1 - row, odd]).astype(jnp.int32)

    def edge_rows(value, edge, length):
        return lax.dynamic_slice_in_dim(value, edge * (value.shape[1] - length), length, axis=1)

    images = [
        jnp.concatenate([edge_rows(v, edge, z.halo) for v in (observed, inverse_variance)])
        for edge in edges
    ]
    *flat, done = prepare(
        z, place, row_kernel, col_kernel, observed, inverse_variance, images
    )
    cols_m, grad_m, tall_m, above_m, below_m, back_m = [flat[i : i + 2] for i in range(0, 12, 2)]
    observed_near, weights_near = flat[12:]
    blocks = [block] + [hop(block, d) for d in range(1, chips)]
    same = jnp.concatenate(blocks, axis=0)
    other = swap(same)

    strips = [
        jnp.concatenate([edge_rows(v, edge, z.rim + z.extra) for v in (same, other)])
        for edge in edges
    ]
    strips = [lax.ppermute(v, "ty", p) for v, p in zip(strips, pairings)]
    images = [lax.ppermute(v, "ty", p) for v, p in zip(images, pairings)]

    table = jnp.concatenate([same[:, 0], other[:, 0]])[:, : z.bands + 1]
    far_table = jnp.stack([v[:, at] for at in (0, z.rim) for v in strips])[..., : z.bands + 1]
    far_table = far_table.reshape(-1, z.bands + 1)
    predicted = inner_call(z, place, table, done, same, other, cols_m, tall_m)
    terms = jax.ShapeDtypeStruct((chips * sources, z.box + z.extra, z.box), F32)
    residual, terms_same, terms_other = outer_call(
        z, terms, place, table, far_table, same, other, *strips, *images, observed_near, weights_near,
        predicted, cols_m, grad_m, above_m, below_m, back_m,
    )

    chip_terms = terms_same + swap(terms_other)
    per_chip = chip_terms.reshape(chips, sources, z.box + z.extra, z.box)
    received = [per_chip[0]] + [hop(per_chip[d], d, back=True) for d in range(1, chips)]
    new_morph, new_sed = pl.pallas_call(
        functools.partial(last_kernel, len(received)),
        out_shape=[
            jax.ShapeDtypeStruct(morph.shape[1:], F32),
            jax.ShapeDtypeStruct(sed.shape[1:], F32),
        ],
        in_specs=[VMEM] * (len(received) + 3),
        out_specs=[VMEM] * 2,
        compiler_params=params(8),
        name="update",
    )(*received, morph[0], sed[0], gamma[0][:, None])
    return residual, new_morph[None], new_sed[None]


def solution(mesh):
    tile = P(None, "ty", "tx")
    source = P("ty", "tx")
    return jax.shard_map(
        body,
        mesh=mesh,
        in_specs=(tile, tile, source, source, source, source, P(), P()),
        out_specs=(tile, source, source),
        check_vma=False,
    )
```

```python
import functools

import jax
import jax.numpy as jnp
from jax import lax
from jax.experimental import pallas as pl
from jax.experimental.pallas import tpu as pltpu
from jax.sharding import PartitionSpec as P

F32 = jnp.float32
BF16 = jnp.bfloat16
VMEM = pl.BlockSpec(memory_space=pltpu.VMEM)
SMEM = pl.BlockSpec(memory_space=pltpu.SMEM)
HBM = pl.BlockSpec(memory_space=pltpu.HBM)
MIB = 1024 * 1024


def params(mebibytes):
    return pltpu.CompilerParams(vmem_limit_bytes=mebibytes * MIB)


def up_to(value, step):
    return -(-value // step) * step


def halves(value):
    high = value.astype(BF16)
    return high, (value - high.astype(F32)).astype(BF16)


def product(left, right):
    dot = functools.partial(jnp.dot, preferred_element_type=F32)
    (lh, ll), (rh, rl) = left, right
    rows = lh.shape[0]
    both = dot(jnp.concatenate([lh, ll], 0), rh)
    return both[:rows] + (dot(lh, rl) + both[rows:])


class Sizes:
    def __init__(self, observed, morph, taps):
        self.bands, self.rows, self.cols = observed
        self.box = morph[-1]
        self.per_tile = self.cols // self.box
        self.taps = taps
        self.reach = (taps - 1) // 2
        self.halo = up_to(self.reach, 8)
        self.rim = up_to(2 * self.reach, 8)
        self.tall = self.rows + 2 * self.halo
        self.near = self.halo + up_to(self.reach, 8)
        self.extra = up_to(self.bands, 8)


def prepare_kernel(z, place, row_ref, col_ref, observed, weights, *out):
    mats, out = out[-20:-8], out[-8:]
    observed_out, weights_out, done, row_taps, col_taps, cycles, turned, sems = out
    cols_m, grad_m, tall_m, above_m, below_m, back_m = [mats[i : i + 2] for i in range(0, 12, 2)]
    copies = [
        pltpu.make_async_copy(observed, observed_out, sems.at[0]),
        pltpu.make_async_copy(weights, weights_out, sems.at[1]),
    ]
    for copy in copies:
        copy.start()

    box = z.box

    row_taps[...] = jnp.zeros(row_taps.shape, F32)
    col_taps[...] = jnp.zeros(col_taps.shape, F32)
    row_taps[: z.bands, : z.taps] = row_ref[...]
    col_taps[: z.bands, : z.taps] = col_ref[...]

    def cycle(ref, band, shift):
        row = pltpu.roll(jnp.broadcast_to(ref[band : band + 1, :], (8, box)), shift % box, 1)
        spread = jnp.broadcast_to(row[:1, :], (box, box))
        return pltpu.roll(spread, 0, 1, stride=1, stride_axis=0)

    def turn(value, count, shift):
        value = pltpu.roll(value, shift % box, 1)
        return jnp.concatenate([value, value], 0)[:count]

    def tap(count, start, shift):
        at = lax.broadcasted_iota(jnp.int32, (count, box), 1)
        at += start - shift - lax.broadcasted_iota(jnp.int32, (count, box), 0)
        return ((at >= 0) & (at < z.taps)).astype(F32).astype(BF16)

    def cut(value, mask):
        return [half * mask for half in halves(value)]

    def keep(pair, band, value, rows=slice(None), lanes=slice(None)):
        for ref, half in zip(pair, value):
            ref[band, rows, lanes] = half

    as_half = lambda mask: mask.astype(F32).astype(BF16)
    at_row = lax.broadcasted_iota(jnp.int32, (box, box), 0)
    at_lane = lax.broadcasted_iota(jnp.int32, (box, box), 1)
    lower, upper = as_half(at_row >= box // 2), as_half(at_row < box // 2)
    right, left = as_half(at_lane >= box // 2), as_half(at_lane < box // 2)
    none = [jnp.zeros((box, box), BF16)] * 2
    whole = [slice(i * box, (i + 1) * box) for i in range(z.per_tile + 1)]
    col_shift = -z.reach
    tall_shift = -z.halo - z.reach
    above_shift = z.rim - z.halo - z.reach
    below_shift = z.tall - z.near - z.halo - z.rows - z.reach
    back_shift = z.halo - z.reach
    flip_shift = lambda shift: shift + 2 * z.reach + back_shift
    apart = {d: tap(box, d * box, col_shift) for d in (-1, 0, 1)}
    tall_mask = tap(z.tall, 0, tall_shift)
    above_mask = tap(z.near, 0, above_shift)
    below_mask = tap(z.near, 0, below_shift)
    back_masks = [tap(z.rows, start, back_shift) for start in range(0, z.tall, box)]
    for band in range(z.bands):
        cycles[band] = cycle(col_taps, band, col_shift)
        cycles[z.bands + band] = cycle(row_taps, band, back_shift)
    for index in range(2 * z.bands):
        turned[index] = cycles[index].T
    for band in range(z.bands):
        block = {d: cut(cycles[band], apart[d]) for d in apart}
        flipped = {d: cut(turned[band], apart[d]) for d in apart}
        for i in range(z.per_tile):
            for j in range(z.per_tile):
                keep(cols_m, band, block.get(j - i, none), whole[i], whole[j])
                keep(grad_m, band, flipped.get(j - i, none), whole[i], whole[j])
        for i in range(z.per_tile):
            edge = none
            if i == 0:
                edge = [p + h * lower for p, h in zip(edge, block[1])]
            if i == z.per_tile - 1:
                edge = [p + h * upper for p, h in zip(edge, block[-1])]
            keep(cols_m, band, edge, whole[z.per_tile], whole[i])
            edge = none
            if i == 0:
                edge = [p + h * right for p, h in zip(edge, flipped[-1])]
            if i == z.per_tile - 1:
                edge = [p + h * left for p, h in zip(edge, flipped[1])]
            keep(grad_m, band, edge, whole[i], whole[z.per_tile])
    for band in range(z.bands):
        value, flip = cycles[z.bands + band], turned[z.bands + band]
        keep(tall_m, band, cut(turn(flip, z.tall, flip_shift(tall_shift)), tall_mask))
        for pair, shift, mask in (
            (above_m, above_shift, above_mask),
            (below_m, below_shift, below_mask),
        ):
            part = cut(turn(flip, z.near, flip_shift(shift)), mask)
            keep(pair, band, [h[:, : z.rim] for h in part])
        for index, mask in enumerate(back_masks):
            start = index * box
            size = min(box, z.tall - start)
            part = [h[:, :size] for h in cut(value, mask)]
            keep(back_m, band, part, lanes=slice(start, start + size))
    for copy in copies:
        copy.wait()
    done[...] = jnp.zeros(done.shape, F32)


def prepare(z, place, row_kernel, col_kernel, observed, weights, after):
    sizes = [
        (z.cols + z.box, z.cols),
        (z.cols, z.cols + z.box),
        (z.tall, z.rows),
        (z.near, z.rim),
        (z.near, z.rim),
        (z.rows, z.tall),
    ]
    return pl.pallas_call(
        functools.partial(prepare_kernel, z),
        out_shape=[jax.ShapeDtypeStruct((z.bands,) + s, BF16) for s in sizes for _ in range(2)]
        + [jax.ShapeDtypeStruct(observed.shape, F32)] * 2
        + [jax.ShapeDtypeStruct((8, 128), F32)],
        in_specs=[SMEM] + [VMEM] * 2 + [HBM] * (2 + len(after)),
        out_specs=[VMEM] * 15,
        scratch_shapes=[pltpu.VMEM((up_to(z.bands, 8), z.box), F32)] * 2
        + [pltpu.VMEM((2 * z.bands, z.box, z.box), F32)] * 2
        + [pltpu.SemaphoreType.DMA((2,))],
        compiler_params=params(8),
        cost_estimate=pl.CostEstimate(flops=10**9, bytes_accessed=10**7, transcendentals=0),
        name="prepare",
    )(place, row_kernel, col_kernel, observed, weights, *after)


def box_of(z, foot, first):
    place = foot.astype(jnp.int32) - first
    inside = (place >= 0) & (place < z.per_tile)
    near = (place >= -1) & (place <= z.per_tile)
    box = jnp.where(inside, place, z.per_tile)
    low = jnp.where(place == -1, z.box // 2, 0)
    high = jnp.where(place == z.per_tile, z.box // 2, z.box)
    return near, pl.ds(pl.multiple_of(box * z.box, z.box), z.box), low, high


def add_sources(z, place, valid, info, offset, source, count, row, model, start, length):
    lane = lax.broadcasted_iota(jnp.int32, (length, z.box), 1)

    def step(k, _):
        near, at, low, high = box_of(z, info[offset + k, z.bands], place[0])

        @pl.when(near)
        def _():
            value = jnp.where((lane >= low) & (lane < high), source[k, row : row + length, :], 0.0)
            for band in range(z.bands):
                model[band, start : start + length, at] += info[offset + k, band] * value

        return 0

    @pl.when(valid)
    def _():
        lax.fori_loop(0, count, step, 0)


def inner_kernel(z, place, info, done, same, other, *refs):
    cols_h, cols_l, tall_h, tall_l, predicted, model, blurred = refs
    half = same.shape[0]
    model[...] = jnp.zeros(model.shape, F32)
    add_sources(z, place, place[3] >= 0, info, 0, same, half, z.extra, model, 0, z.rows)
    add_sources(z, place, place[3] >= 0, info, half, other, half, z.extra, model, 0, z.rows)
    for band in range(z.bands):
        blurred[band] = product(halves(model[band]), (cols_h[band], cols_l[band]))
    for band in range(z.bands):
        predicted[band] = product((tall_h[band], tall_l[band]), halves(blurred[band]))


def outer_kernel(z, place, info, info_far, same, other, far_0, far_1, images_0, images_1, *refs):
    observed, weights, predicted = refs[:3]
    cols_m, grad_m, above_m, below_m, back_m = [refs[i : i + 2] for i in range(3, 13, 2)]
    residual_hbm, terms_same, terms_other = refs[13:16]
    residual, model, gradient, backrows, blurred, sems = refs[16:]
    half = same.shape[0]
    model[...] = jnp.zeros(model.shape, F32)
    count = 2 * half
    odd = place[3]
    for which, far in enumerate((far_0, far_1)):
        above = (odd != which) & (place[1] > 0)
        below = (odd == which) & (place[2] > 0)
        first, last = (2 + which) * count, which * count
        add_sources(z, place, above, info_far, first, far, count, 0, model, 0, z.rim)
        add_sources(z, place, below, info_far, last, far, count, z.extra, model, z.rim, z.rim)
    stores = []
    rest = z.tall - z.near
    middle = slice(z.halo, z.halo + z.rows)
    for band in range(z.bands):
        blurred[band] = product(halves(model[band]), (cols_m[0][band], cols_m[1][band]))
    for band in range(z.bands):
        first = product((above_m[0][band], above_m[1][band]), halves(blurred[band, : z.rim]))
        last = product((below_m[0][band], below_m[1][band]), halves(blurred[band, z.rim :]))
        whole = jnp.concatenate(
            [
                predicted[band, : z.near] + first,
                predicted[band, z.near : rest],
                predicted[band, rest:] + last,
            ],
            0,
        )
        residual[band, middle] = weights[band] * (observed[band] - whole[middle])
        store = pltpu.make_async_copy(
            residual.at[band, middle], residual_hbm.at[band], sems.at[band]
        )
        store.start()
        stores.append(store)
        images = [
            [ref[part + band] for ref in (images_0, images_1)] for part in (0, z.bands)
        ]
        seen, weight = [jnp.where(odd > 0, a, b) for a, b in images]
        residual[band, : z.halo] = weight * (seen - whole[: z.halo])
        seen, weight = [jnp.where(odd > 0, b, a) for a, b in images]
        residual[band, z.halo + z.rows :] = weight * (seen - whole[z.halo + z.rows :])
    for band in range(z.bands):
        backrows[band] = product((back_m[0][band], back_m[1][band]), halves(residual[band]))
    for band in range(z.bands):
        gradient[band] = product(halves(backrows[band]), (grad_m[0][band], grad_m[1][band]))

    lane = lax.broadcasted_iota(jnp.int32, (z.rows, z.box), 1)
    for side, (source, terms) in enumerate(((same, terms_same), (other, terms_other))):

        def step(k, _, side=side, source=source, terms=terms):
            at_info = side * half + k
            near, at, low, high = box_of(z, info[at_info, z.bands], place[0])

            @pl.when(near)
            def _():
                keep = (lane >= low) & (lane < high)
                shape = jnp.where(keep, source[k, z.extra : z.extra + z.rows, :], 0.0)
                total = jnp.zeros((z.rows, z.box), F32)
                for band in range(z.bands):
                    value = gradient[band, :, at]
                    total += info[at_info, band] * value
                    terms[k, z.box + band : z.box + band + 1, :] = jnp.sum(
                        shape * value, axis=0, keepdims=True
                    )
                terms[k, : z.box, :] = jnp.where(keep, total, 0.0)
                unused = terms.shape[1] - z.box - z.bands
                if unused:
                    terms[k, z.box + z.bands :, :] = jnp.zeros((unused, z.box), F32)

            @pl.when(jnp.logical_not(near))
            def _():
                terms[k] = jnp.zeros(terms.shape[1:], F32)

            return 0

        lax.fori_loop(0, half, step, 0)
    for store in stores:
        store.wait()


def inner_call(z, place, table, done, same, other, cols_m, tall_m):
    return pl.pallas_call(
        functools.partial(inner_kernel, z),
        out_shape=jax.ShapeDtypeStruct((z.bands, z.tall, z.cols), F32),
        in_specs=[SMEM] * 2 + [VMEM] * 7,
        out_specs=VMEM,
        scratch_shapes=[
            pltpu.VMEM((z.bands, z.rows, z.cols + z.box), F32),
            pltpu.VMEM((z.bands, z.rows, z.cols), F32),
        ],
        compiler_params=params(8),
        cost_estimate=pl.CostEstimate(flops=10**9, bytes_accessed=10**7, transcendentals=0),
        name="inner_rows",
    )(place, table, done, same, other, *cols_m, *tall_m)


def outer_call(z, terms, place, table, far_table, same, other, far_0, far_1, images_0, images_1, observed,
               weights, predicted, cols_m, grad_m, above_m, below_m, back_m):
    return pl.pallas_call(
        functools.partial(outer_kernel, z),
        out_shape=[jax.ShapeDtypeStruct(observed.shape, F32), terms, terms],
        in_specs=[SMEM] * 3 + [VMEM] * 19,
        out_specs=[HBM, VMEM, VMEM],
        scratch_shapes=[
            pltpu.VMEM((z.bands, z.tall, z.cols), F32),
            pltpu.VMEM((z.bands, 2 * z.rim, z.cols + z.box), F32),
            pltpu.VMEM((z.bands, z.rows, z.cols + z.box), F32),
            pltpu.VMEM((z.bands, z.rows, z.cols), F32),
            pltpu.VMEM((z.bands, 2 * z.rim, z.cols), F32),
            pltpu.SemaphoreType.DMA((z.bands,)),
        ],
        compiler_params=params(12),
        name="whole_step",
    )(
        place, table, far_table, same, other, far_0, far_1, images_0, images_1, observed, weights,
        predicted, *cols_m, *grad_m, *above_m, *below_m, *back_m,
    )


def last_kernel(count, *refs):
    received, (morph, sed, gamma, new_morph, new_sed) = refs[:count], refs[count:]
    box = morph.shape[1]
    bands = sed.shape[1]
    for k in range(morph.shape[0]):
        total = received[0][k]
        for ref in received[1:]:
            total += ref[k]
        mine = morph[k]
        spectrum = sed[k : k + 1, :]
        step = gamma[k : k + 1, :]
        step_morph = step / jnp.sum(spectrum * spectrum, axis=1, keepdims=True)
        new_morph[k] = jnp.maximum(mine + step_morph * total[:box], 0.0)
        squares = jnp.sum(jnp.sum(mine * mine, axis=0, keepdims=True), axis=1, keepdims=True)
        step_sed = step / jnp.sqrt(squares)
        sums = jnp.sum(total[box : box + bands], axis=1, keepdims=True)
        eye = lax.broadcasted_iota(jnp.int32, (bands, bands), 0) == lax.broadcasted_iota(
            jnp.int32, (bands, bands), 1
        )
        sed_grad = jnp.sum(jnp.where(eye, sums, 0.0), axis=0, keepdims=True)
        new_sed[k : k + 1, :] = jnp.maximum(spectrum + step_sed * sed_grad, 0.0)


def body(observed, inverse_variance, sed, morph, foot_block, gamma, row_kernel, col_kernel):
    z = Sizes(observed.shape, morph.shape, row_kernel.shape[1])
    sources = morph.shape[1]
    tiles, tile_rows = lax.axis_size("tx"), lax.axis_size("ty")
    chips = tiles // 2
    paired = chips & (chips - 1) == 0

    def hop(value, distance, back=False):
        if paired:
            pairs = [(i, i ^ (2 * distance)) for i in range(tiles)]
        else:
            pairs = [(i, (i + 2 * distance) % tiles) for i in range(tiles)]
            pairs = [(j, i) for i, j in pairs] if back else pairs
        return lax.ppermute(value, "tx", pairs)

    def swap(value):
        return lax.ppermute(value, "tx", [(i, i ^ 1) for i in range(tiles)])

    row = lax.axis_index("ty")
    odd = row % 2

    pairings = [[(i, i + 1) for i in range(start, tile_rows - 1, 2)] for start in (0, 1)]
    pairings = [pairs + [(j, i) for i, j in pairs] for pairs in pairings]
    edges = [jnp.where(odd == start, 1, 0).astype(jnp.int32) for start in (0, 1)]
    first = lax.axis_index("tx") * z.per_tile
    place = jnp.stack([first, row, tile_rows - 1 - row, odd]).astype(jnp.int32)

    def edge_rows(value, edge, length):
        return lax.dynamic_slice_in_dim(value, edge * (value.shape[1] - length), length, axis=1)

    images = [
        jnp.concatenate([edge_rows(v, edge, z.halo) for v in (observed, inverse_variance)])
        for edge in edges
    ]
    sed_tied, images[0], images[1] = lax.optimization_barrier((sed, images[0], images[1]))
    ends = ((0, 0), (z.extra, z.extra), (0, 0))
    block = jnp.pad(morph[0], ends)
    for start in (0, z.extra + z.box):
        rows = (start, 2 * z.extra + z.box - 1 - start)
        foot = foot_block[0][:, None, None].astype(F32)
        block += jnp.pad(sed_tied[0][:, None], ((0, 0), rows, (0, z.box - z.bands)))
        block += jnp.pad(foot, ((0, 0), rows, (z.bands, z.box - z.bands - 1)))
    blocks = [block] + [hop(block, d) for d in range(1, chips)]
    same = jnp.concatenate(blocks, axis=0)
    other = swap(same)

    *flat, done = prepare(
        z, place, row_kernel, col_kernel, observed, inverse_variance, [other, *images]
    )
    cols_m, grad_m, tall_m, above_m, below_m, back_m = [flat[i : i + 2] for i in range(0, 12, 2)]
    observed_near, weights_near = flat[12:]
    strips = [
        jnp.concatenate([edge_rows(v, edge, z.rim + z.extra) for v in (same, other)])
        for edge in edges
    ]
    strips = [lax.ppermute(v, "ty", p) for v, p in zip(strips, pairings)]
    images = [lax.ppermute(v, "ty", p) for v, p in zip(images, pairings)]

    table = jnp.concatenate([same[:, 0], other[:, 0]])[:, : z.bands + 1]
    far_table = jnp.stack([v[:, at] for at in (0, z.rim) for v in strips])[..., : z.bands + 1]
    far_table = far_table.reshape(-1, z.bands + 1)
    predicted = inner_call(z, place, table, done, same, other, cols_m, tall_m)
    terms = jax.ShapeDtypeStruct((chips * sources, z.box + z.extra, z.box), F32)
    residual, terms_same, terms_other = outer_call(
        z, terms, place, table, far_table, same, other, *strips, *images, observed_near, weights_near,
        predicted, cols_m, grad_m, above_m, below_m, back_m,
    )

    chip_terms = terms_same + swap(terms_other)
    per_chip = chip_terms.reshape(chips, sources, z.box + z.extra, z.box)
    received = [per_chip[0]] + [hop(per_chip[d], d, back=True) for d in range(1, chips)]
    new_morph, new_sed = pl.pallas_call(
        functools.partial(last_kernel, len(received)),
        out_shape=[
            jax.ShapeDtypeStruct(morph.shape[1:], F32),
            jax.ShapeDtypeStruct(sed.shape[1:], F32),
        ],
        in_specs=[VMEM] * (len(received) + 3),
        out_specs=[VMEM] * 2,
        compiler_params=params(8),
        name="update",
    )(*received, morph[0], sed[0], gamma[0][:, None])
    return residual, new_morph[None], new_sed[None]


def solution(mesh):
    tile = P(None, "ty", "tx")
    source = P("ty", "tx")
    return jax.shard_map(
        body,
        mesh=mesh,
        in_specs=(tile, tile, source, source, source, source, P(), P()),
        out_specs=(tile, source, source),
        check_vma=False,
    )
```

```python
import functools

import jax
import jax.numpy as jnp
from jax import lax
from jax.experimental import pallas as pl
from jax.experimental.pallas import tpu as pltpu
from jax.sharding import PartitionSpec as P

F32 = jnp.float32
BF16 = jnp.bfloat16
VMEM = pl.BlockSpec(memory_space=pltpu.VMEM)
SMEM = pl.BlockSpec(memory_space=pltpu.SMEM)
HBM = pl.BlockSpec(memory_space=pltpu.HBM)
MIB = 1024 * 1024


def params(mebibytes):
    return pltpu.CompilerParams(vmem_limit_bytes=mebibytes * MIB)


def up_to(value, step):
    return -(-value // step) * step


def halves(value):
    high = value.astype(BF16)
    return high, (value - high.astype(F32)).astype(BF16)


def product(left, right):
    dot = functools.partial(jnp.dot, preferred_element_type=F32)
    (lh, ll), (rh, rl) = left, right
    rows = lh.shape[0]
    both = dot(jnp.concatenate([lh, ll], 0), rh)
    return both[:rows] + (dot(lh, rl) + both[rows:])


class Sizes:
    def __init__(self, observed, morph, taps):
        self.bands, self.rows, self.cols = observed
        self.box = morph[-1]
        self.per_tile = self.cols // self.box
        self.taps = taps
        self.reach = (taps - 1) // 2
        self.halo = up_to(self.reach, 8)
        self.rim = up_to(2 * self.reach, 8)
        self.tall = self.rows + 2 * self.halo
        self.near = self.halo + up_to(self.reach, 8)
        self.extra = up_to(self.bands + 1, 8)
        self.slots = 2 * morph[1]


def pack_kernel(z, morph, sed, foot, out):
    row = lax.broadcasted_iota(jnp.int32, (z.extra, z.box), 0)
    for k in range(out.shape[0]):
        info = jnp.where(row == z.bands, foot[k : k + 1, :].astype(F32), 0.0)
        for band in range(z.bands):
            info = jnp.where(row == band, sed[k : k + 1, band : band + 1], info)
        out[k, : z.extra, :] = info
        out[k, z.extra : z.extra + z.box, :] = morph[k]
        out[k, z.extra + z.box :, :] = info


def make_matrices(z, row_ref, col_ref, mats, row_taps, col_taps, cycles, turned):
    cols_m, grad_m, tall_m, above_m, below_m, back_m = [mats[i : i + 2] for i in range(0, 12, 2)]
    box = z.box

    row_taps[...] = jnp.zeros(row_taps.shape, F32)
    col_taps[...] = jnp.zeros(col_taps.shape, F32)
    row_taps[: z.bands, : z.taps] = row_ref[...]
    col_taps[: z.bands, : z.taps] = col_ref[...]

    def cycle(ref, band, shift):
        row = pltpu.roll(jnp.broadcast_to(ref[band : band + 1, :], (8, box)), shift % box, 1)
        spread = jnp.broadcast_to(row[:1, :], (box, box))
        return pltpu.roll(spread, 0, 1, stride=1, stride_axis=0)

    def turn(value, count, shift):
        value = pltpu.roll(value, shift % box, 1)
        return jnp.concatenate([value, value], 0)[:count]

    def tap(count, start, shift):
        at = lax.broadcasted_iota(jnp.int32, (count, box), 1)
        at += start - shift - lax.broadcasted_iota(jnp.int32, (count, box), 0)
        return ((at >= 0) & (at < z.taps)).astype(F32).astype(BF16)

    def cut(value, mask):
        return [half * mask for half in halves(value)]

    def keep(pair, band, value, rows=slice(None), lanes=slice(None)):
        for ref, half in zip(pair, value):
            ref[band, rows, lanes] = half

    as_half = lambda mask: mask.astype(F32).astype(BF16)
    at_row = lax.broadcasted_iota(jnp.int32, (box, box), 0)
    at_lane = lax.broadcasted_iota(jnp.int32, (box, box), 1)
    lower, upper = as_half(at_row >= box // 2), as_half(at_row < box // 2)
    right, left = as_half(at_lane >= box // 2), as_half(at_lane < box // 2)
    none = [jnp.zeros((box, box), BF16)] * 2
    whole = [slice(i * box, (i + 1) * box) for i in range(z.per_tile + 1)]
    col_shift = -z.reach
    tall_shift = -z.halo - z.reach
    above_shift = z.rim - z.halo - z.reach
    below_shift = z.tall - z.near - z.halo - z.rows - z.reach
    back_shift = z.halo - z.reach
    flip_shift = lambda shift: shift + 2 * z.reach + back_shift
    apart = {d: tap(box, d * box, col_shift) for d in (-1, 0, 1)}
    tall_mask = tap(z.tall, 0, tall_shift)
    above_mask = tap(z.near, 0, above_shift)
    below_mask = tap(z.near, 0, below_shift)
    back_masks = [tap(z.rows, start, back_shift) for start in range(0, z.tall, box)]
    for band in range(z.bands):
        cycles[band] = cycle(col_taps, band, col_shift)
        cycles[z.bands + band] = cycle(row_taps, band, back_shift)
    for index in range(2 * z.bands):
        turned[index] = cycles[index].T
    for band in range(z.bands):
        block = {d: cut(cycles[band], apart[d]) for d in apart}
        flipped = {d: cut(turned[band], apart[d]) for d in apart}
        for i in range(z.per_tile):
            for j in range(z.per_tile):
                keep(cols_m, band, block.get(j - i, none), whole[i], whole[j])
                keep(grad_m, band, flipped.get(j - i, none), whole[i], whole[j])
        for i in range(z.per_tile):
            edge = none
            if i == 0:
                edge = [p + h * lower for p, h in zip(edge, block[1])]
            if i == z.per_tile - 1:
                edge = [p + h * upper for p, h in zip(edge, block[-1])]
            keep(cols_m, band, edge, whole[z.per_tile], whole[i])
            edge = none
            if i == 0:
                edge = [p + h * right for p, h in zip(edge, flipped[-1])]
            if i == z.per_tile - 1:
                edge = [p + h * left for p, h in zip(edge, flipped[1])]
            keep(grad_m, band, edge, whole[i], whole[z.per_tile])
    for band in range(z.bands):
        value, flip = cycles[z.bands + band], turned[z.bands + band]
        keep(tall_m, band, cut(turn(flip, z.tall, flip_shift(tall_shift)), tall_mask))
        for pair, shift, mask in (
            (above_m, above_shift, above_mask),
            (below_m, below_shift, below_mask),
        ):
            part = cut(turn(flip, z.near, flip_shift(shift)), mask)
            keep(pair, band, [h[:, : z.rim] for h in part])
        for index, mask in enumerate(back_masks):
            start = index * box
            size = min(box, z.tall - start)
            part = [h[:, :size] for h in cut(value, mask)]
            keep(back_m, band, part, lanes=slice(start, start + size))


def box_of(z, foot, first):
    place = foot.astype(jnp.int32) - first
    inside = (place >= 0) & (place < z.per_tile)
    near = (place >= -1) & (place <= z.per_tile)
    box = jnp.where(inside, place, z.per_tile)
    low = jnp.where(place == -1, z.box // 2, 0)
    high = jnp.where(place == z.per_tile, z.box // 2, z.box)
    return near, pl.ds(pl.multiple_of(box * z.box, z.box), z.box), low, high


def add_sources(z, place, info, offset, source, count, row, model, start, length):
    lane = lax.broadcasted_iota(jnp.int32, (length, z.box), 1)

    def step(k, _):
        near, at, low, high = box_of(z, info[offset + k, z.bands], place[0])

        @pl.when(near)
        def _():
            value = jnp.where((lane >= low) & (lane < high), source[k, row : row + length, :], 0.0)
            for band in range(z.bands):
                model[band, start : start + length, at] += info[offset + k, band] * value

        return 0

    lax.fori_loop(0, count, step, 0)


def edge_strips(z, rows, columns, first):
    count = columns.shape[0]
    at = columns - first.astype(F32)
    own = ((at >= 0.0) & (at < z.per_tile)).astype(F32)
    lane = lax.broadcasted_iota(jnp.int32, at.shape, 1)
    side = (at == jnp.where(lane >= z.box // 2, -1.0, float(z.per_tile))).astype(F32)
    index = lax.broadcasted_iota(jnp.int32, (count, count, 1), 0)
    earlier = (lax.broadcasted_iota(jnp.int32, (count, count, 1), 1) < index).astype(F32)
    masks = []
    for group in (own, side):
        rank = jnp.sum(earlier * group[None], axis=1)
        masks += [jnp.where(rank == slot, group, 0.0) for slot in range(z.slots)]
    return [
        jnp.stack([jnp.sum(mask[:, None, :] * part, axis=0) for mask in masks]) for part in rows
    ]


def inner_kernel(z, place, info, row_ref, col_ref, observed, weights, same, other, *refs):
    cols_h, cols_l, grad_h, grad_l, above_h, above_l, below_h, below_l, back_h, back_l = refs[:10]
    observed_out, weights_out, predicted = refs[10:13]
    tall_h, tall_l, row_taps, col_taps, cycles, turned, model, blurred, sems = refs[13:]
    copies = [
        pltpu.make_async_copy(observed, observed_out, sems.at[0]),
        pltpu.make_async_copy(weights, weights_out, sems.at[1]),
    ]
    for copy in copies:
        copy.start()
    mats = (cols_h, cols_l, grad_h, grad_l, tall_h, tall_l)
    mats += (above_h, above_l, below_h, below_l, back_h, back_l)
    make_matrices(z, row_ref, col_ref, mats, row_taps, col_taps, cycles, turned)
    half = same.shape[0]
    model[...] = jnp.zeros(model.shape, F32)
    add_sources(z, place, info, 0, same, half, z.extra, model, 0, z.rows)
    add_sources(z, place, info, half, other, half, z.extra, model, 0, z.rows)
    for band in range(z.bands):
        blurred[band] = product(halves(model[band]), (cols_h[band], cols_l[band]))
    for band in range(z.bands):
        predicted[band] = product((tall_h[band], tall_l[band]), halves(blurred[band]))
    for copy in copies:
        copy.wait()


def outer_kernel(z, place, info, same, other, far_1, far_0, images_0, images_1, *refs):
    observed, weights, predicted = refs[:3]
    cols_m, grad_m, above_m, below_m, back_m = [refs[i : i + 2] for i in range(3, 13, 2)]
    residual_hbm, terms_same, terms_other = refs[13:16]
    residual, model, gradient, backrows, blurred, sems = refs[16:]
    half = same.shape[0]
    odd = place[3]
    first = place[0].astype(F32)
    for pairing, far in enumerate((far_0, far_1)):
        start = pl.multiple_of(jnp.where(odd == pairing, z.rim, 0), 8)
        rows = pl.ds(start, z.rim)
        upper = pl.ds(pl.multiple_of(jnp.where(odd == pairing, z.extra, 0), 8), z.rim)
        ends = pl.ds(pl.multiple_of(jnp.where(odd == pairing, 0, z.rim), 8), z.extra)
        strips = [far[slot, upper, :] for slot in range(2 * z.slots)]
        notes = [far[slot, ends, :] for slot in range(2 * z.slots)]
        columns = [note[z.bands : z.bands + 1, :] - first for note in notes]
        for j in range(z.per_tile + 1):
            own = j < z.per_tile
            used = range(z.slots) if own else range(z.slots, 2 * z.slots)
            masks = [(columns[k] == j).astype(F32) for k in used] if own else [1.0] * z.slots
            for band in range(z.bands):
                total = 0.0
                for k, mask in zip(used, masks):
                    total += (notes[k][band : band + 1, :] * mask) * strips[k]
                model[band, rows, j * z.box : (j + 1) * z.box] = total
    stores = []
    rest = z.tall - z.near
    middle = slice(z.halo, z.halo + z.rows)
    for band in range(z.bands):
        blurred[band] = product(halves(model[band]), (cols_m[0][band], cols_m[1][band]))
    for band in range(z.bands):
        first = product((above_m[0][band], above_m[1][band]), halves(blurred[band, : z.rim]))
        last = product((below_m[0][band], below_m[1][band]), halves(blurred[band, z.rim :]))
        whole = jnp.concatenate(
            [
                predicted[band, : z.near] + first,
                predicted[band, z.near : rest],
                predicted[band, rest:] + last,
            ],
            0,
        )
        residual[band, middle] = weights[band] * (observed[band] - whole[middle])
        store = pltpu.make_async_copy(
            residual.at[band, middle], residual_hbm.at[band], sems.at[band]
        )
        store.start()
        stores.append(store)
        images = [
            [ref[part + band] for ref in (images_0, images_1)] for part in (0, z.bands)
        ]
        seen, weight = [jnp.where(odd > 0, a, b) for a, b in images]
        residual[band, : z.halo] = weight * (seen - whole[: z.halo])
        seen, weight = [jnp.where(odd > 0, b, a) for a, b in images]
        residual[band, z.halo + z.rows :] = weight * (seen - whole[z.halo + z.rows :])
    for band in range(z.bands):
        backrows[band] = product((back_m[0][band], back_m[1][band]), halves(residual[band]))
    for band in range(z.bands):
        gradient[band] = product(halves(backrows[band]), (grad_m[0][band], grad_m[1][band]))

    lane = lax.broadcasted_iota(jnp.int32, (z.rows, z.box), 1)
    for side, (source, terms) in enumerate(((same, terms_same), (other, terms_other))):

        def step(k, _, side=side, source=source, terms=terms):
            at_info = side * half + k
            near, at, low, high = box_of(z, info[at_info, z.bands], place[0])

            @pl.when(near)
            def _():
                keep = (lane >= low) & (lane < high)
                shape = jnp.where(keep, source[k, z.extra : z.extra + z.rows, :], 0.0)
                total = jnp.zeros((z.rows, z.box), F32)
                for band in range(z.bands):
                    value = gradient[band, :, at]
                    total += info[at_info, band] * value
                    terms[k, z.box + band : z.box + band + 1, :] = jnp.sum(
                        shape * value, axis=0, keepdims=True
                    )
                terms[k, : z.box, :] = jnp.where(keep, total, 0.0)
                unused = terms.shape[1] - z.box - z.bands
                if unused:
                    terms[k, z.box + z.bands :, :] = jnp.zeros((unused, z.box), F32)

            @pl.when(jnp.logical_not(near))
            def _():
                terms[k] = jnp.zeros(terms.shape[1:], F32)

            return 0

        lax.fori_loop(0, half, step, 0)
    for store in stores:
        store.wait()


def inner_call(z, place, table, row_kernel, col_kernel, observed, weights, same, other):
    sizes = [
        (z.cols + z.box, z.cols),
        (z.cols, z.cols + z.box),
        (z.near, z.rim),
        (z.near, z.rim),
        (z.rows, z.tall),
    ]
    matrices = [jax.ShapeDtypeStruct((z.bands,) + s, BF16) for s in sizes for _ in range(2)]
    *flat, observed, weights, predicted = pl.pallas_call(
        functools.partial(inner_kernel, z),
        out_shape=matrices
        + [jax.ShapeDtypeStruct(observed.shape, F32)] * 2
        + [jax.ShapeDtypeStruct((z.bands, z.tall, z.cols), F32)],
        in_specs=[SMEM] * 2 + [VMEM] * 2 + [HBM] * 2 + [VMEM] * 2,
        out_specs=[VMEM] * 13,
        scratch_shapes=[pltpu.VMEM((z.bands, z.tall, z.rows), BF16)] * 2
        + [pltpu.VMEM((up_to(z.bands, 8), z.box), F32)] * 2
        + [pltpu.VMEM((2 * z.bands, z.box, z.box), F32)] * 2
        + [
            pltpu.VMEM((z.bands, z.rows, z.cols + z.box), F32),
            pltpu.VMEM((z.bands, z.rows, z.cols), F32),
            pltpu.SemaphoreType.DMA((2,)),
        ],
        compiler_params=params(16),
        cost_estimate=pl.CostEstimate(flops=10**9, bytes_accessed=10**7, transcendentals=0),
        name="inner_rows",
    )(place, table, row_kernel, col_kernel, observed, weights, same, other)
    return [flat[i : i + 2] for i in range(0, 10, 2)], observed, weights, predicted


def outer_call(z, terms, place, table, same, other, far_0, far_1, images_0, images_1, observed,
               weights, predicted, cols_m, grad_m, above_m, below_m, back_m):
    return pl.pallas_call(
        functools.partial(outer_kernel, z),
        out_shape=[jax.ShapeDtypeStruct(observed.shape, F32), terms, terms],
        in_specs=[SMEM] * 2 + [VMEM] * 19,
        out_specs=[HBM, VMEM, VMEM],
        scratch_shapes=[
            pltpu.VMEM((z.bands, z.tall, z.cols), F32),
            pltpu.VMEM((z.bands, 2 * z.rim, z.cols + z.box), F32),
            pltpu.VMEM((z.bands, z.rows, z.cols + z.box), F32),
            pltpu.VMEM((z.bands, z.rows, z.cols), F32),
            pltpu.VMEM((z.bands, 2 * z.rim, z.cols), F32),
            pltpu.SemaphoreType.DMA((z.bands,)),
        ],
        compiler_params=params(12),
        name="whole_step",
    )(
        place, table, same, other, far_0, far_1, images_0, images_1, observed, weights,
        predicted, *cols_m, *grad_m, *above_m, *below_m, *back_m,
    )


def last_kernel(count, *refs):
    received, (morph, sed, gamma, new_morph, new_sed) = refs[:count], refs[count:]
    box = morph.shape[1]
    bands = sed.shape[1]
    for k in range(morph.shape[0]):
        total = received[0][k]
        for ref in received[1:]:
            total += ref[k]
        mine = morph[k]
        spectrum = sed[k : k + 1, :]
        step = gamma[k : k + 1, :]
        step_morph = step / jnp.sum(spectrum * spectrum, axis=1, keepdims=True)
        new_morph[k] = jnp.maximum(mine + step_morph * total[:box], 0.0)
        squares = jnp.sum(jnp.sum(mine * mine, axis=0, keepdims=True), axis=1, keepdims=True)
        step_sed = step / jnp.sqrt(squares)
        sums = jnp.sum(total[box : box + bands], axis=1, keepdims=True)
        eye = lax.broadcasted_iota(jnp.int32, (bands, bands), 0) == lax.broadcasted_iota(
            jnp.int32, (bands, bands), 1
        )
        sed_grad = jnp.sum(jnp.where(eye, sums, 0.0), axis=0, keepdims=True)
        new_sed[k : k + 1, :] = jnp.maximum(spectrum + step_sed * sed_grad, 0.0)


def body(observed, inverse_variance, sed, morph, foot_block, gamma, row_kernel, col_kernel):
    z = Sizes(observed.shape, morph.shape, row_kernel.shape[1])
    sources = morph.shape[1]
    tiles, tile_rows = lax.axis_size("tx"), lax.axis_size("ty")
    chips = tiles // 2
    paired = chips & (chips - 1) == 0

    def hop(value, distance, back=False):
        if paired:
            pairs = [(i, i ^ (2 * distance)) for i in range(tiles)]
        else:
            pairs = [(i, (i + 2 * distance) % tiles) for i in range(tiles)]
            pairs = [(j, i) for i, j in pairs] if back else pairs
        return lax.ppermute(value, "tx", pairs)

    def swap(value):
        return lax.ppermute(value, "tx", [(i, i ^ 1) for i in range(tiles)])

    row = lax.axis_index("ty")
    odd = row & 1

    pairings = [[(i, i + 1) for i in range(start, tile_rows - 1, 2)] for start in (0, 1)]
    pairings = [pairs + [(j, i) for i, j in pairs] for pairs in pairings]
    edges = [1 - odd, odd]
    first = lax.axis_index("tx") * z.per_tile
    place = jnp.stack([first, row, tile_rows - 1 - row, odd]).astype(jnp.int32)

    def edge_rows(value, edge, length):
        start = edge * (value.shape[1] - length)
        size = (value.shape[0], length, value.shape[2])
        return lax.dynamic_slice(value, (0, start, 0), size, allow_negative_indices=False)

    images = [
        jnp.concatenate([edge_rows(v, edge, z.halo) for v in (observed, inverse_variance)])
        for edge in edges
    ]
    sed_tied, images[0], images[1] = lax.optimization_barrier((sed, images[0], images[1]))
    block = pl.pallas_call(
        functools.partial(pack_kernel, z),
        out_shape=jax.ShapeDtypeStruct((sources, z.box + 2 * z.extra, z.box), F32),
        in_specs=[VMEM] * 3,
        out_specs=VMEM,
        compiler_params=params(4),
        name="pack",
    )(morph[0], sed_tied[0], foot_block[0][:, None])
    order = [*range(1, chips, 2), *range(2, chips, 2)]
    blocks = [block] + [hop(block, d) for d in order]
    same = jnp.concatenate(blocks, axis=0)
    other = swap(same)

    table = jnp.concatenate([same[:, : z.bands + 1, 0], other[:, : z.bands + 1, 0]])
    rows = [
        jnp.concatenate([edge_rows(v, edge, z.rim + z.extra) for v in (same, other)])
        for edge in edges
    ]
    columns = jnp.concatenate([same[:, z.bands], other[:, z.bands]])
    strips = edge_strips(z, rows, columns, first)
    strips = [lax.ppermute(v, "ty", p) for v, p in zip(strips, pairings)]
    images = [lax.ppermute(v, "ty", p) for v, p in zip(images, pairings)]

    matrices, observed_near, weights_near, predicted = inner_call(
        z, place, table, row_kernel, col_kernel, observed, inverse_variance, same, other
    )
    cols_m, grad_m, above_m, below_m, back_m = matrices
    terms = jax.ShapeDtypeStruct((chips * sources, z.box + z.extra, z.box), F32)
    residual, terms_same, terms_other = outer_call(
        z, terms, place, table, same, other, *strips[::-1], *images, observed_near, weights_near,
        predicted, cols_m, grad_m, above_m, below_m, back_m,
    )

    chip_terms = terms_same + swap(terms_other)
    per_chip = chip_terms.reshape(chips, sources, z.box + z.extra, z.box)
    received = [per_chip[0]]
    received += [hop(per_chip[at], d, back=True) for at, d in enumerate(order, 1)]
    new_morph, new_sed = pl.pallas_call(
        functools.partial(last_kernel, len(received)),
        out_shape=[
            jax.ShapeDtypeStruct(morph.shape[1:], F32),
            jax.ShapeDtypeStruct(sed.shape[1:], F32),
        ],
        in_specs=[VMEM] * (len(received) + 3),
        out_specs=[VMEM] * 2,
        compiler_params=params(8),
        name="update",
    )(*received, morph[0], sed[0], gamma[0][:, None])
    return residual, new_morph[None], new_sed[None]


def solution(mesh):
    tile = P(None, "ty", "tx")
    source = P("ty", "tx")
    return jax.shard_map(
        body,
        mesh=mesh,
        in_specs=(tile, tile, source, source, source, source, P(), P()),
        out_specs=(tile, source, source),
        check_vma=False,
    )
```

```python
import functools

import jax
import jax.numpy as jnp
from jax import lax
from jax.experimental import pallas as pl
from jax.experimental.pallas import tpu as pltpu
from jax.sharding import PartitionSpec as P

F32 = jnp.float32
BF16 = jnp.bfloat16
VMEM = pl.BlockSpec(memory_space=pltpu.VMEM)
SMEM = pl.BlockSpec(memory_space=pltpu.SMEM)
HBM = pl.BlockSpec(memory_space=pltpu.HBM)
MIB = 1024 * 1024


def params(mebibytes):
    return pltpu.CompilerParams(vmem_limit_bytes=mebibytes * MIB)


def up_to(value, step):
    return -(-value // step) * step


def halves(value):
    high = value.astype(BF16)
    return high, (value - high.astype(F32)).astype(BF16)


def product(left, right):
    dot = functools.partial(jnp.dot, preferred_element_type=F32)
    (lh, ll), (rh, rl) = left, right
    rows = lh.shape[0]
    both = dot(jnp.concatenate([lh, ll], 0), rh)
    return both[:rows] + (dot(lh, rl) + both[rows:])


class Sizes:
    def __init__(self, observed, morph, taps):
        self.bands, self.rows, self.cols = observed
        self.box = morph[-1]
        self.per_tile = self.cols // self.box
        self.taps = taps
        self.reach = (taps - 1) // 2
        self.halo = up_to(self.reach, 8)
        self.rim = up_to(2 * self.reach, 8)
        self.tall = self.rows + 2 * self.halo
        self.near = self.halo + up_to(self.reach, 8)
        self.extra = up_to(self.bands + 1, 8)
        self.slots = 2 * morph[1]


def pack_kernel(z, morph, sed, foot, out):
    row = lax.broadcasted_iota(jnp.int32, (z.extra, z.box), 0)
    for k in range(out.shape[0]):
        info = jnp.where(row == z.bands, foot[k : k + 1, :].astype(F32), 0.0)
        for band in range(z.bands):
            info = jnp.where(row == band, sed[k : k + 1, band : band + 1], info)
        out[k, : z.extra, :] = info
        out[k, z.extra : z.extra + z.box, :] = morph[k]
        out[k, z.extra + z.box :, :] = info


def make_matrices(z, row_ref, col_ref, mats, row_taps, col_taps, cycles, turned):
    cols_m, grad_m, tall_m, above_m, below_m, back_m = [mats[i : i + 2] for i in range(0, 12, 2)]
    box = z.box

    row_taps[...] = jnp.zeros(row_taps.shape, F32)
    col_taps[...] = jnp.zeros(col_taps.shape, F32)
    row_taps[: z.bands, : z.taps] = row_ref[...]
    col_taps[: z.bands, : z.taps] = col_ref[...]

    def cycle(ref, band, shift):
        row = pltpu.roll(jnp.broadcast_to(ref[band : band + 1, :], (8, box)), shift % box, 1)
        spread = jnp.broadcast_to(row[:1, :], (box, box))
        return pltpu.roll(spread, 0, 1, stride=1, stride_axis=0)

    def turn(value, count, shift):
        value = pltpu.roll(value, shift % box, 1)
        return jnp.concatenate([value, value], 0)[:count]

    def tap(count, start, shift):
        at = lax.broadcasted_iota(jnp.int32, (count, box), 1)
        at += start - shift - lax.broadcasted_iota(jnp.int32, (count, box), 0)
        return ((at >= 0) & (at < z.taps)).astype(F32).astype(BF16)

    def cut(value, mask):
        return [half * mask for half in halves(value)]

    def keep(pair, band, value, rows=slice(None), lanes=slice(None)):
        for ref, half in zip(pair, value):
            ref[band, rows, lanes] = half

    as_half = lambda mask: mask.astype(F32).astype(BF16)
    at_row = lax.broadcasted_iota(jnp.int32, (box, box), 0)
    at_lane = lax.broadcasted_iota(jnp.int32, (box, box), 1)
    lower, upper = as_half(at_row >= box // 2), as_half(at_row < box // 2)
    right, left = as_half(at_lane >= box // 2), as_half(at_lane < box // 2)
    none = [jnp.zeros((box, box), BF16)] * 2
    whole = [slice(i * box, (i + 1) * box) for i in range(z.per_tile + 1)]
    col_shift = -z.reach
    tall_shift = -z.halo - z.reach
    above_shift = z.rim - z.halo - z.reach
    below_shift = z.tall - z.near - z.halo - z.rows - z.reach
    back_shift = z.halo - z.reach
    flip_shift = lambda shift: shift + 2 * z.reach + back_shift
    apart = {d: tap(box, d * box, col_shift) for d in (-1, 0, 1)}
    tall_mask = tap(z.tall, 0, tall_shift)
    above_mask = tap(z.near, 0, above_shift)
    below_mask = tap(z.near, 0, below_shift)
    back_masks = [tap(z.rows, start, back_shift) for start in range(0, z.tall, box)]
    for band in range(z.bands):
        cycles[band] = cycle(col_taps, band, col_shift)
        cycles[z.bands + band] = cycle(row_taps, band, back_shift)
    for index in range(2 * z.bands):
        turned[index] = cycles[index].T
    for band in range(z.bands):
        block = {d: cut(cycles[band], apart[d]) for d in apart}
        for i in range(z.per_tile):
            for j in range(z.per_tile):
                keep(cols_m, band, block.get(j - i, none), whole[i], whole[j])
            edge = none
            if i == 0:
                edge = [p + h * lower for p, h in zip(edge, block[1])]
            if i == z.per_tile - 1:
                edge = [p + h * upper for p, h in zip(edge, block[-1])]
            keep(cols_m, band, edge, whole[z.per_tile], whole[i])
        flip = turned[z.bands + band]
        keep(tall_m, band, cut(turn(flip, z.tall, flip_shift(tall_shift)), tall_mask))

    def later_columns(band):
        flipped = {d: cut(turned[band], apart[d]) for d in apart}
        for i in range(z.per_tile):
            for j in range(z.per_tile):
                keep(grad_m, band, flipped.get(j - i, none), whole[i], whole[j])
            edge = none
            if i == 0:
                edge = [p + h * right for p, h in zip(edge, flipped[-1])]
            if i == z.per_tile - 1:
                edge = [p + h * left for p, h in zip(edge, flipped[1])]
            keep(grad_m, band, edge, whole[i], whole[z.per_tile])

    def later_rows(band):
        value, flip = cycles[z.bands + band], turned[z.bands + band]
        for pair, shift, mask in (
            (above_m, above_shift, above_mask),
            (below_m, below_shift, below_mask),
        ):
            part = cut(turn(flip, z.near, flip_shift(shift)), mask)
            keep(pair, band, [h[:, : z.rim] for h in part])
        for index, mask in enumerate(back_masks):
            start = index * box
            size = min(box, z.tall - start)
            part = [h[:, :size] for h in cut(value, mask)]
            keep(back_m, band, part, lanes=slice(start, start + size))

    return later_columns, later_rows


def box_of(z, foot, first):
    place = foot.astype(jnp.int32) - first
    inside = (place >= 0) & (place < z.per_tile)
    near = (place >= -1) & (place <= z.per_tile)
    box = jnp.where(inside, place, z.per_tile)
    low = jnp.where(place == -1, z.box // 2, 0)
    high = jnp.where(place == z.per_tile, z.box // 2, z.box)
    return near, pl.ds(pl.multiple_of(box * z.box, z.box), z.box), low, high


def model_rows(z, place, strips, notes, model, rows):
    first = place[0].astype(F32)
    columns = [note[z.bands : z.bands + 1, :] - first for note in notes]
    for j in range(z.per_tile + 1):
        own = j < z.per_tile
        used = range(z.slots) if own else range(z.slots, 2 * z.slots)
        masks = [(columns[k] == j).astype(F32) for k in used] if own else [1.0] * z.slots
        for band in range(z.bands):
            total = 0.0
            for k, mask in zip(used, masks):
                total += (notes[k][band : band + 1, :] * mask) * strips[k]
            model[band, rows, j * z.box : (j + 1) * z.box] = total


def window_slots(z, rows, columns, first):
    count = columns.shape[0]
    at = columns - first.astype(F32)
    own = ((at >= 0.0) & (at < z.per_tile)).astype(F32)
    lane = lax.broadcasted_iota(jnp.int32, at.shape, 1)
    side = (at == jnp.where(lane >= z.box // 2, -1.0, float(z.per_tile))).astype(F32)
    index = lax.broadcasted_iota(jnp.int32, (count, count, 1), 0)
    earlier = (lax.broadcasted_iota(jnp.int32, (count, count, 1), 1) < index).astype(F32)
    masks = []
    for group in (own, side):
        rank = jnp.sum(earlier * group[None], axis=1)
        masks += [jnp.where(rank == slot, group, 0.0) for slot in range(z.slots)]
    return jnp.stack([jnp.sum(mask[:, None, :] * rows, axis=0) for mask in masks])


def inner_kernel(z, place, row_ref, col_ref, observed, weights, slots, *refs):
    cols_h, cols_l, grad_h, grad_l, above_h, above_l, below_h, below_l, back_h, back_l = refs[:10]
    observed_out, weights_out, predicted = refs[10:13]
    tall_h, tall_l, row_taps, col_taps, cycles, turned, model, blurred, sems = refs[13:]
    copies = [
        pltpu.make_async_copy(observed, observed_out, sems.at[0]),
        pltpu.make_async_copy(weights, weights_out, sems.at[1]),
    ]
    for copy in copies:
        copy.start()
    mats = (cols_h, cols_l, grad_h, grad_l, tall_h, tall_l)
    mats += (above_h, above_l, below_h, below_l, back_h, back_l)
    later_columns, later_rows = make_matrices(
        z, row_ref, col_ref, mats, row_taps, col_taps, cycles, turned
    )
    used = range(2 * z.slots)
    strips = [slots[slot, z.extra : z.extra + z.rows, :] for slot in used]
    notes = [slots[slot, : z.extra, :] for slot in used]
    model_rows(z, place, strips, notes, model, slice(None))
    for band in range(z.bands):
        blurred[band] = product(halves(model[band]), (cols_h[band], cols_l[band]))
        later_columns(band)
    for band in range(z.bands):
        predicted[band] = product((tall_h[band], tall_l[band]), halves(blurred[band]))
        later_rows(band)
    for copy in copies:
        copy.wait()


def outer_kernel(z, place, info, same, other, far_0, far_1, images_0, images_1, *refs):
    observed, weights, predicted = refs[:3]
    cols_m, grad_m, above_m, below_m, back_m = [refs[i : i + 2] for i in range(3, 13, 2)]
    residual_hbm, terms_same, terms_other = refs[13:16]
    residual, model, gradient, backrows, blurred, sems = refs[16:]
    half = same.shape[0]
    odd = place[3]
    for pairing, far in enumerate((far_0, far_1)):
        start = pl.multiple_of(jnp.where(odd == pairing, z.rim, 0), 8)
        rows = pl.ds(start, z.rim)
        upper = pl.ds(pl.multiple_of(jnp.where(odd == pairing, z.extra, 0), 8), z.rim)
        ends = pl.ds(pl.multiple_of(jnp.where(odd == pairing, 0, z.rim), 8), z.extra)
        strips = [far[slot, upper, :] for slot in range(2 * z.slots)]
        notes = [far[slot, ends, :] for slot in range(2 * z.slots)]
        model_rows(z, place, strips, notes, model, rows)
    stores = []
    rest = z.tall - z.near
    middle = slice(z.halo, z.halo + z.rows)
    for band in range(z.bands):
        blurred[band] = product(halves(model[band]), (cols_m[0][band], cols_m[1][band]))
    for band in range(z.bands):
        first = product((above_m[0][band], above_m[1][band]), halves(blurred[band, : z.rim]))
        last = product((below_m[0][band], below_m[1][band]), halves(blurred[band, z.rim :]))
        whole = jnp.concatenate(
            [
                predicted[band, : z.near] + first,
                predicted[band, z.near : rest],
                predicted[band, rest:] + last,
            ],
            0,
        )
        residual[band, middle] = weights[band] * (observed[band] - whole[middle])
        store = pltpu.make_async_copy(
            residual.at[band, middle], residual_hbm.at[band], sems.at[band]
        )
        store.start()
        stores.append(store)
        images = [
            [ref[part + band] for ref in (images_0, images_1)] for part in (0, z.bands)
        ]
        seen, weight = [jnp.where(odd > 0, a, b) for a, b in images]
        residual[band, : z.halo] = weight * (seen - whole[: z.halo])
        seen, weight = [jnp.where(odd > 0, b, a) for a, b in images]
        residual[band, z.halo + z.rows :] = weight * (seen - whole[z.halo + z.rows :])
    for band in range(z.bands):
        backrows[band] = product((back_m[0][band], back_m[1][band]), halves(residual[band]))
    for band in range(z.bands):
        gradient[band] = product(halves(backrows[band]), (grad_m[0][band], grad_m[1][band]))

    lane = lax.broadcasted_iota(jnp.int32, (z.rows, z.box), 1)
    for side, (source, terms) in enumerate(((same, terms_same), (other, terms_other))):

        def step(k, _, side=side, source=source, terms=terms):
            at_info = side * half + k
            near, at, low, high = box_of(z, info[at_info, z.bands], place[0])

            @pl.when(near)
            def _():
                keep = (lane >= low) & (lane < high)
                shape = jnp.where(keep, source[k, z.extra : z.extra + z.rows, :], 0.0)
                total = jnp.zeros((z.rows, z.box), F32)
                for band in range(z.bands):
                    value = gradient[band, :, at]
                    total += info[at_info, band] * value
                    terms[k, z.box + band : z.box + band + 1, :] = jnp.sum(
                        shape * value, axis=0, keepdims=True
                    )
                terms[k, : z.box, :] = jnp.where(keep, total, 0.0)
                unused = terms.shape[1] - z.box - z.bands
                if unused:
                    terms[k, z.box + z.bands :, :] = jnp.zeros((unused, z.box), F32)

            @pl.when(jnp.logical_not(near))
            def _():
                terms[k] = jnp.zeros(terms.shape[1:], F32)

            return 0

        lax.fori_loop(0, half, step, 0)
    for store in stores:
        store.wait()


def inner_call(z, place, row_kernel, col_kernel, observed, weights, slots):
    sizes = [
        (z.cols + z.box, z.cols),
        (z.cols, z.cols + z.box),
        (z.near, z.rim),
        (z.near, z.rim),
        (z.rows, z.tall),
    ]
    matrices = [jax.ShapeDtypeStruct((z.bands,) + s, BF16) for s in sizes for _ in range(2)]
    *flat, observed, weights, predicted = pl.pallas_call(
        functools.partial(inner_kernel, z),
        out_shape=matrices
        + [jax.ShapeDtypeStruct(observed.shape, F32)] * 2
        + [jax.ShapeDtypeStruct((z.bands, z.tall, z.cols), F32)],
        in_specs=[SMEM] + [VMEM] * 2 + [HBM] * 2 + [VMEM],
        out_specs=[VMEM] * 13,
        scratch_shapes=[pltpu.VMEM((z.bands, z.tall, z.rows), BF16)] * 2
        + [pltpu.VMEM((up_to(z.bands, 8), z.box), F32)] * 2
        + [pltpu.VMEM((2 * z.bands, z.box, z.box), F32)] * 2
        + [
            pltpu.VMEM((z.bands, z.rows, z.cols + z.box), F32),
            pltpu.VMEM((z.bands, z.rows, z.cols), F32),
            pltpu.SemaphoreType.DMA((2,)),
        ],
        compiler_params=params(16),
        cost_estimate=pl.CostEstimate(flops=10**9, bytes_accessed=10**7, transcendentals=0),
        name="inner_rows",
    )(place, row_kernel, col_kernel, observed, weights, slots)
    return [flat[i : i + 2] for i in range(0, 10, 2)], observed, weights, predicted


def outer_call(z, terms, place, table, same, other, far_0, far_1, images_0, images_1, observed,
               weights, predicted, cols_m, grad_m, above_m, below_m, back_m):
    return pl.pallas_call(
        functools.partial(outer_kernel, z),
        out_shape=[jax.ShapeDtypeStruct(observed.shape, F32), terms, terms],
        in_specs=[SMEM] * 2 + [VMEM] * 19,
        out_specs=[HBM, VMEM, VMEM],
        scratch_shapes=[
            pltpu.VMEM((z.bands, z.tall, z.cols), F32),
            pltpu.VMEM((z.bands, 2 * z.rim, z.cols + z.box), F32),
            pltpu.VMEM((z.bands, z.rows, z.cols + z.box), F32),
            pltpu.VMEM((z.bands, z.rows, z.cols), F32),
            pltpu.VMEM((z.bands, 2 * z.rim, z.cols), F32),
            pltpu.SemaphoreType.DMA((z.bands,)),
        ],
        compiler_params=params(12),
        name="whole_step",
    )(
        place, table, same, other, far_0, far_1, images_0, images_1, observed, weights,
        predicted, *cols_m, *grad_m, *above_m, *below_m, *back_m,
    )


def last_kernel(count, *refs):
    received, (morph, sed, gamma, new_morph, new_sed) = refs[:count], refs[count:]
    box = morph.shape[1]
    bands = sed.shape[1]
    for k in range(morph.shape[0]):
        total = received[0][k]
        for ref in received[1:]:
            total += ref[k]
        mine = morph[k]
        spectrum = sed[k : k + 1, :]
        step = gamma[k : k + 1, :]
        step_morph = step / jnp.sum(spectrum * spectrum, axis=1, keepdims=True)
        new_morph[k] = jnp.maximum(mine + step_morph * total[:box], 0.0)
        squares = jnp.sum(jnp.sum(mine * mine, axis=0, keepdims=True), axis=1, keepdims=True)
        step_sed = step / jnp.sqrt(squares)
        sums = jnp.sum(total[box : box + bands], axis=1, keepdims=True)
        eye = lax.broadcasted_iota(jnp.int32, (bands, bands), 0) == lax.broadcasted_iota(
            jnp.int32, (bands, bands), 1
        )
        sed_grad = jnp.sum(jnp.where(eye, sums, 0.0), axis=0, keepdims=True)
        new_sed[k : k + 1, :] = jnp.maximum(spectrum + step_sed * sed_grad, 0.0)


def body(observed, inverse_variance, sed, morph, foot_block, gamma, row_kernel, col_kernel):
    z = Sizes(observed.shape, morph.shape, row_kernel.shape[1])
    sources = morph.shape[1]
    tiles, tile_rows = lax.axis_size("tx"), lax.axis_size("ty")
    chips = tiles // 2
    paired = chips & (chips - 1) == 0

    def hop(value, distance, back=False):
        if paired:
            pairs = [(i, i ^ (2 * distance)) for i in range(tiles)]
        else:
            pairs = [(i, (i + 2 * distance) % tiles) for i in range(tiles)]
            pairs = [(j, i) for i, j in pairs] if back else pairs
        return lax.ppermute(value, "tx", pairs)

    def swap(value):
        return lax.ppermute(value, "tx", [(i, i ^ 1) for i in range(tiles)])

    row = lax.axis_index("ty")
    odd = row & 1

    pairings = [[(i, i + 1) for i in range(start, tile_rows - 1, 2)] for start in (0, 1)]
    pairings = [pairs + [(j, i) for i, j in pairs] for pairs in pairings]
    edges = [1 - odd, odd]
    first = lax.axis_index("tx") * z.per_tile
    place = jnp.stack([first, row, tile_rows - 1 - row, odd]).astype(jnp.int32)

    def edge_rows(value, edge, length):
        start = edge * (value.shape[1] - length)
        size = (value.shape[0], length, value.shape[2])
        return lax.dynamic_slice(value, (0, start, 0), size, allow_negative_indices=False)

    images = [
        jnp.concatenate([edge_rows(v, edge, z.halo) for v in (observed, inverse_variance)])
        for edge in edges
    ]
    sed_tied, images[0], images[1] = lax.optimization_barrier((sed, images[0], images[1]))
    block = pl.pallas_call(
        functools.partial(pack_kernel, z),
        out_shape=jax.ShapeDtypeStruct((sources, z.box + 2 * z.extra, z.box), F32),
        in_specs=[VMEM] * 3,
        out_specs=VMEM,
        compiler_params=params(4),
        name="pack",
    )(morph[0], sed_tied[0], foot_block[0][:, None])
    order = [*range(1, chips, 2), *range(2, chips, 2)]
    blocks = [block] + [hop(block, d) for d in order]
    same = jnp.concatenate(blocks, axis=0)
    other = swap(same)

    table = jnp.concatenate([same[:, : z.bands + 1, 0], other[:, : z.bands + 1, 0]])
    columns = jnp.concatenate([same[:, z.bands], other[:, z.bands]])
    slots = window_slots(z, jnp.concatenate([same, other]), columns, first)
    strips = [edge_rows(slots, edge, z.rim + z.extra) for edge in edges]
    strips = [lax.ppermute(v, "ty", p) for v, p in zip(strips, pairings)]
    images = [lax.ppermute(v, "ty", p) for v, p in zip(images, pairings)]

    matrices, observed_near, weights_near, predicted = inner_call(
        z, place, row_kernel, col_kernel, observed, inverse_variance, slots
    )
    cols_m, grad_m, above_m, below_m, back_m = matrices
    terms = jax.ShapeDtypeStruct((chips * sources, z.box + z.extra, z.box), F32)
    residual, terms_same, terms_other = outer_call(
        z, terms, place, table, same, other, *strips, *images, observed_near, weights_near,
        predicted, cols_m, grad_m, above_m, below_m, back_m,
    )

    chip_terms = terms_same + swap(terms_other)
    per_chip = chip_terms.reshape(chips, sources, z.box + z.extra, z.box)
    received = [per_chip[0]]
    received += [hop(per_chip[at], d, back=True) for at, d in enumerate(order, 1)]
    new_morph, new_sed = pl.pallas_call(
        functools.partial(last_kernel, len(received)),
        out_shape=[
            jax.ShapeDtypeStruct(morph.shape[1:], F32),
            jax.ShapeDtypeStruct(sed.shape[1:], F32),
        ],
        in_specs=[VMEM] * (len(received) + 3),
        out_specs=[VMEM] * 2,
        compiler_params=params(8),
        name="update",
    )(*received, morph[0], sed[0], gamma[0][:, None])
    return residual, new_morph[None], new_sed[None]


def solution(mesh):
    tile = P(None, "ty", "tx")
    source = P("ty", "tx")
    return jax.shard_map(
        body,
        mesh=mesh,
        in_specs=(tile, tile, source, source, source, source, P(), P()),
        out_specs=(tile, source, source),
        check_vma=False,
    )
```

```python
import functools

import jax
import jax.numpy as jnp
from jax import lax
from jax.experimental import pallas as pl
from jax.experimental.pallas import tpu as pltpu
from jax.sharding import PartitionSpec as P

F32 = jnp.float32
BF16 = jnp.bfloat16
VMEM = pl.BlockSpec(memory_space=pltpu.VMEM)
SMEM = pl.BlockSpec(memory_space=pltpu.SMEM)
HBM = pl.BlockSpec(memory_space=pltpu.HBM)
MIB = 1024 * 1024


def params(mebibytes):
    return pltpu.CompilerParams(vmem_limit_bytes=mebibytes * MIB)


def up_to(value, step):
    return -(-value // step) * step


def halves(value):
    high = value.astype(BF16)
    return high, (value - high.astype(F32)).astype(BF16)


def product(left, right):
    dot = functools.partial(jnp.dot, preferred_element_type=F32)
    (lh, ll), (rh, rl) = left, right
    rows = lh.shape[0]
    both = dot(jnp.concatenate([lh, ll], 0), rh)
    return both[:rows] + (dot(lh, rl) + both[rows:])


class Sizes:
    def __init__(self, observed, morph, taps):
        self.bands, self.rows, self.cols = observed
        self.box = morph[-1]
        self.per_tile = self.cols // self.box
        self.taps = taps
        self.reach = (taps - 1) // 2
        self.halo = up_to(self.reach, 8)
        self.rim = up_to(2 * self.reach, 8)
        self.tall = self.rows + 2 * self.halo
        self.near = self.halo + up_to(self.reach, 8)
        self.extra = up_to(self.bands + 1, 8)
        self.slots = 2 * morph[1]


def pack_kernel(z, morph, sed, foot, out):
    row = lax.broadcasted_iota(jnp.int32, (z.extra, z.box), 0)
    for k in range(out.shape[0]):
        info = jnp.where(row == z.bands, foot[k : k + 1, :].astype(F32), 0.0)
        for band in range(z.bands):
            info = jnp.where(row == band, sed[k : k + 1, band : band + 1], info)
        out[k, : z.extra, :] = info
        out[k, z.extra : z.extra + z.box, :] = morph[k]
        out[k, z.extra + z.box :, :] = info


def make_matrices(z, row_ref, col_ref, mats, row_taps, col_taps, cycles, turned):
    cols_m, grad_m, tall_m, above_m, below_m, back_m = [mats[i : i + 2] for i in range(0, 12, 2)]
    box = z.box

    row_taps[...] = jnp.zeros(row_taps.shape, F32)
    col_taps[...] = jnp.zeros(col_taps.shape, F32)
    row_taps[: z.bands, : z.taps] = row_ref[...]
    col_taps[: z.bands, : z.taps] = col_ref[...]

    def cycle(ref, band, shift):
        row = pltpu.roll(jnp.broadcast_to(ref[band : band + 1, :], (8, box)), shift % box, 1)
        spread = jnp.broadcast_to(row[:1, :], (box, box))
        return pltpu.roll(spread, 0, 1, stride=1, stride_axis=0)

    def turn(value, count, shift):
        value = pltpu.roll(value, shift % box, 1)
        return jnp.concatenate([value, value], 0)[:count]

    def tap(count, start, shift):
        at = lax.broadcasted_iota(jnp.int32, (count, box), 1)
        at += start - shift - lax.broadcasted_iota(jnp.int32, (count, box), 0)
        return ((at >= 0) & (at < z.taps)).astype(F32).astype(BF16)

    def cut(value, mask):
        return [half * mask for half in halves(value)]

    def keep(pair, band, value, rows=slice(None), lanes=slice(None)):
        for ref, half in zip(pair, value):
            ref[band, rows, lanes] = half

    as_half = lambda mask: mask.astype(F32).astype(BF16)
    at_row = lax.broadcasted_iota(jnp.int32, (box, box), 0)
    at_lane = lax.broadcasted_iota(jnp.int32, (box, box), 1)
    lower, upper = as_half(at_row >= box // 2), as_half(at_row < box // 2)
    right, left = as_half(at_lane >= box // 2), as_half(at_lane < box // 2)
    none = [jnp.zeros((box, box), BF16)] * 2
    whole = [slice(i * box, (i + 1) * box) for i in range(z.per_tile + 1)]
    col_shift = -z.reach
    tall_shift = -z.halo - z.reach
    above_shift = z.rim - z.halo - z.reach
    below_shift = z.tall - z.near - z.halo - z.rows - z.reach
    back_shift = z.halo - z.reach
    flip_shift = lambda shift: shift + 2 * z.reach + back_shift
    apart = {d: tap(box, d * box, col_shift) for d in (-1, 0, 1)}
    tall_mask = tap(z.tall, 0, tall_shift)
    above_mask = tap(z.near, 0, above_shift)
    below_mask = tap(z.near, 0, below_shift)
    back_masks = [tap(z.rows, start, back_shift) for start in range(0, z.tall, box)]
    for band in range(z.bands):
        cycles[band] = cycle(col_taps, band, col_shift)
        cycles[z.bands + band] = cycle(row_taps, band, back_shift)
    for index in range(2 * z.bands):
        turned[index] = cycles[index].T
    for band in range(z.bands):
        block = {d: cut(cycles[band], apart[d]) for d in apart}
        for i in range(z.per_tile):
            for j in range(z.per_tile):
                keep(cols_m, band, block.get(j - i, none), whole[i], whole[j])
            edge = none
            if i == 0:
                edge = [p + h * lower for p, h in zip(edge, block[1])]
            if i == z.per_tile - 1:
                edge = [p + h * upper for p, h in zip(edge, block[-1])]
            keep(cols_m, band, edge, whole[z.per_tile], whole[i])
        flip = turned[z.bands + band]
        keep(tall_m, band, cut(turn(flip, z.tall, flip_shift(tall_shift)), tall_mask))

    def later_columns(band):
        flipped = {d: cut(turned[band], apart[d]) for d in apart}
        for i in range(z.per_tile):
            for j in range(z.per_tile):
                keep(grad_m, band, flipped.get(j - i, none), whole[i], whole[j])
            edge = none
            if i == 0:
                edge = [p + h * right for p, h in zip(edge, flipped[-1])]
            if i == z.per_tile - 1:
                edge = [p + h * left for p, h in zip(edge, flipped[1])]
            keep(grad_m, band, edge, whole[i], whole[z.per_tile])

    def later_rows(band):
        value, flip = cycles[z.bands + band], turned[z.bands + band]
        for pair, shift, mask in (
            (above_m, above_shift, above_mask),
            (below_m, below_shift, below_mask),
        ):
            part = cut(turn(flip, z.near, flip_shift(shift)), mask)
            keep(pair, band, [h[:, : z.rim] for h in part])
        for index, mask in enumerate(back_masks):
            start = index * box
            size = min(box, z.tall - start)
            part = [h[:, :size] for h in cut(value, mask)]
            keep(back_m, band, part, lanes=slice(start, start + size))

    return later_columns, later_rows


def box_of(z, foot, first):
    place = foot.astype(jnp.int32) - first
    inside = (place >= 0) & (place < z.per_tile)
    near = (place >= -1) & (place <= z.per_tile)
    box = jnp.where(inside, place, z.per_tile)
    low = jnp.where(place == -1, z.box // 2, 0)
    high = jnp.where(place == z.per_tile, z.box // 2, z.box)
    return near, pl.ds(pl.multiple_of(box * z.box, z.box), z.box), low, high


def model_rows(z, place, strips, notes, model, rows):
    first = place[0].astype(F32)
    columns = [note[z.bands : z.bands + 1, :] - first for note in notes]
    for j in range(z.per_tile + 1):
        own = j < z.per_tile
        used = range(z.slots) if own else range(z.slots, 2 * z.slots)
        masks = [(columns[k] == j).astype(F32) for k in used] if own else [1.0] * z.slots
        for band in range(z.bands):
            total = 0.0
            for k, mask in zip(used, masks):
                total += (notes[k][band : band + 1, :] * mask) * strips[k]
            model[band, rows, j * z.box : (j + 1) * z.box] = total


def window_slots(z, rows, columns, first):
    count = columns.shape[0]
    at = columns - first.astype(F32)
    own = ((at >= 0.0) & (at < z.per_tile)).astype(F32)
    lane = lax.broadcasted_iota(jnp.int32, at.shape, 1)
    side = (at == jnp.where(lane >= z.box // 2, -1.0, float(z.per_tile))).astype(F32)
    index = lax.broadcasted_iota(jnp.int32, (count, count, 1), 0)
    earlier = (lax.broadcasted_iota(jnp.int32, (count, count, 1), 1) < index).astype(F32)
    masks = []
    for group in (own, side):
        rank = jnp.sum(earlier * group[None], axis=1)
        masks += [jnp.where(rank == slot, group, 0.0) for slot in range(z.slots)]
    return jnp.stack([jnp.sum(mask[:, None, :] * rows, axis=0) for mask in masks])


def inner_kernel(z, place, row_ref, col_ref, observed, weights, slots, *refs):
    cols_h, cols_l, grad_h, grad_l, above_h, above_l, below_h, below_l, back_h, back_l = refs[:10]
    observed_out, weights_out, predicted = refs[10:13]
    tall_h, tall_l, row_taps, col_taps, cycles, turned, model, blurred, sems = refs[13:]
    copies = [
        pltpu.make_async_copy(observed, observed_out, sems.at[0]),
        pltpu.make_async_copy(weights, weights_out, sems.at[1]),
    ]
    for copy in copies:
        copy.start()
    mats = (cols_h, cols_l, grad_h, grad_l, tall_h, tall_l)
    mats += (above_h, above_l, below_h, below_l, back_h, back_l)
    later_columns, later_rows = make_matrices(
        z, row_ref, col_ref, mats, row_taps, col_taps, cycles, turned
    )
    used = range(2 * z.slots)
    strips = [slots[slot, z.extra : z.extra + z.rows, :] for slot in used]
    notes = [slots[slot, : z.extra, :] for slot in used]
    model_rows(z, place, strips, notes, model, slice(None))
    for band in range(z.bands):
        blurred[band] = product(halves(model[band]), (cols_h[band], cols_l[band]))
        later_columns(band)
    for band in range(z.bands):
        predicted[band] = product((tall_h[band], tall_l[band]), halves(blurred[band]))
        later_rows(band)
    for copy in copies:
        copy.wait()


def outer_kernel(z, place, info, same, other, far_0, far_1, images_0, images_1, *refs):
    observed, weights, predicted = refs[:3]
    cols_m, grad_m, above_m, below_m, back_m = [refs[i : i + 2] for i in range(3, 13, 2)]
    residual_hbm, terms_same, terms_other = refs[13:16]
    residual, model, gradient, backrows, blurred, sems = refs[16:]
    half = same.shape[0]
    odd = place[3]
    for pairing, far in enumerate((far_0, far_1)):
        start = pl.multiple_of(jnp.where(odd == pairing, z.rim, 0), 8)
        rows = pl.ds(start, z.rim)
        upper = pl.ds(pl.multiple_of(jnp.where(odd == pairing, z.extra, 0), 8), z.rim)
        ends = pl.ds(pl.multiple_of(jnp.where(odd == pairing, 0, z.rim), 8), z.extra)
        strips = [far[slot, upper, :] for slot in range(2 * z.slots)]
        notes = [far[slot, ends, :] for slot in range(2 * z.slots)]
        model_rows(z, place, strips, notes, model, rows)
    stores = []
    rest = z.tall - z.near
    middle = slice(z.halo, z.halo + z.rows)
    for band in range(z.bands):
        blurred[band] = product(halves(model[band]), (cols_m[0][band], cols_m[1][band]))
    for band in range(z.bands):
        first = product((above_m[0][band], above_m[1][band]), halves(blurred[band, : z.rim]))
        last = product((below_m[0][band], below_m[1][band]), halves(blurred[band, z.rim :]))
        whole = jnp.concatenate(
            [
                predicted[band, : z.near] + first,
                predicted[band, z.near : rest],
                predicted[band, rest:] + last,
            ],
            0,
        )
        residual[band, middle] = weights[band] * (observed[band] - whole[middle])
        store = pltpu.make_async_copy(
            residual.at[band, middle], residual_hbm.at[band], sems.at[band]
        )
        store.start()
        stores.append(store)
        images = [
            [ref[part + band] for ref in (images_0, images_1)] for part in (0, z.bands)
        ]
        seen, weight = [jnp.where(odd > 0, a, b) for a, b in images]
        residual[band, : z.halo] = weight * (seen - whole[: z.halo])
        seen, weight = [jnp.where(odd > 0, b, a) for a, b in images]
        residual[band, z.halo + z.rows :] = weight * (seen - whole[z.halo + z.rows :])
    for band in range(z.bands):
        backrows[band] = product((back_m[0][band], back_m[1][band]), halves(residual[band]))
    for band in range(z.bands):
        gradient[band] = product(halves(backrows[band]), (grad_m[0][band], grad_m[1][band]))

    lane = lax.broadcasted_iota(jnp.int32, (z.rows, z.box), 1)
    for side, (source, terms) in enumerate(((same, terms_same), (other, terms_other))):

        def step(k, _, side=side, source=source, terms=terms):
            at_info = side * half + k
            near, at, low, high = box_of(z, info[at_info, z.bands], place[0])

            @pl.when(near)
            def _():
                keep = (lane >= low) & (lane < high)
                shape = jnp.where(keep, source[k, z.extra : z.extra + z.rows, :], 0.0)
                total = jnp.zeros((z.rows, z.box), F32)
                for band in range(z.bands):
                    value = gradient[band, :, at]
                    total += info[at_info, band] * value
                    terms[k, z.box + band : z.box + band + 1, :] = jnp.sum(
                        shape * value, axis=0, keepdims=True
                    )
                terms[k, : z.box, :] = jnp.where(keep, total, 0.0)
                unused = terms.shape[1] - z.box - z.bands
                if unused:
                    terms[k, z.box + z.bands :, :] = jnp.zeros((unused, z.box), F32)

            @pl.when(jnp.logical_not(near))
            def _():
                terms[k] = jnp.zeros(terms.shape[1:], F32)

            return 0

        for k in range(half):
            step(k, 0)
    for store in stores:
        store.wait()


def inner_call(z, place, row_kernel, col_kernel, observed, weights, slots):
    sizes = [
        (z.cols + z.box, z.cols),
        (z.cols, z.cols + z.box),
        (z.near, z.rim),
        (z.near, z.rim),
        (z.rows, z.tall),
    ]
    matrices = [jax.ShapeDtypeStruct((z.bands,) + s, BF16) for s in sizes for _ in range(2)]
    *flat, observed, weights, predicted = pl.pallas_call(
        functools.partial(inner_kernel, z),
        out_shape=matrices
        + [jax.ShapeDtypeStruct(observed.shape, F32)] * 2
        + [jax.ShapeDtypeStruct((z.bands, z.tall, z.cols), F32)],
        in_specs=[SMEM] + [VMEM] * 2 + [HBM] * 2 + [VMEM],
        out_specs=[VMEM] * 13,
        scratch_shapes=[pltpu.VMEM((z.bands, z.tall, z.rows), BF16)] * 2
        + [pltpu.VMEM((up_to(z.bands, 8), z.box), F32)] * 2
        + [pltpu.VMEM((2 * z.bands, z.box, z.box), F32)] * 2
        + [
            pltpu.VMEM((z.bands, z.rows, z.cols + z.box), F32),
            pltpu.VMEM((z.bands, z.rows, z.cols), F32),
            pltpu.SemaphoreType.DMA((2,)),
        ],
        compiler_params=params(16),
        cost_estimate=pl.CostEstimate(flops=10**9, bytes_accessed=10**7, transcendentals=0),
        name="inner_rows",
    )(place, row_kernel, col_kernel, observed, weights, slots)
    return [flat[i : i + 2] for i in range(0, 10, 2)], observed, weights, predicted


def outer_call(z, terms, place, table, same, other, far_0, far_1, images_0, images_1, observed,
               weights, predicted, cols_m, grad_m, above_m, below_m, back_m):
    return pl.pallas_call(
        functools.partial(outer_kernel, z),
        out_shape=[jax.ShapeDtypeStruct(observed.shape, F32), terms, terms],
        in_specs=[SMEM] * 2 + [VMEM] * 19,
        out_specs=[HBM, VMEM, VMEM],
        scratch_shapes=[
            pltpu.VMEM((z.bands, z.tall, z.cols), F32),
            pltpu.VMEM((z.bands, 2 * z.rim, z.cols + z.box), F32),
            pltpu.VMEM((z.bands, z.rows, z.cols + z.box), F32),
            pltpu.VMEM((z.bands, z.rows, z.cols), F32),
            pltpu.VMEM((z.bands, 2 * z.rim, z.cols), F32),
            pltpu.SemaphoreType.DMA((z.bands,)),
        ],
        compiler_params=params(12),
        name="whole_step",
    )(
        place, table, same, other, far_0, far_1, images_0, images_1, observed, weights,
        predicted, *cols_m, *grad_m, *above_m, *below_m, *back_m,
    )


def last_kernel(count, *refs):
    received, (morph, sed, gamma, new_morph, new_sed) = refs[:count], refs[count:]
    box = morph.shape[1]
    bands = sed.shape[1]
    for k in range(morph.shape[0]):
        total = received[0][k]
        for ref in received[1:]:
            total += ref[k]
        mine = morph[k]
        spectrum = sed[k : k + 1, :]
        step = gamma[k : k + 1, :]
        step_morph = step / jnp.sum(spectrum * spectrum, axis=1, keepdims=True)
        new_morph[k] = jnp.maximum(mine + step_morph * total[:box], 0.0)
        squares = jnp.sum(jnp.sum(mine * mine, axis=0, keepdims=True), axis=1, keepdims=True)
        step_sed = step / jnp.sqrt(squares)
        sums = jnp.sum(total[box : box + bands], axis=1, keepdims=True)
        eye = lax.broadcasted_iota(jnp.int32, (bands, bands), 0) == lax.broadcasted_iota(
            jnp.int32, (bands, bands), 1
        )
        sed_grad = jnp.sum(jnp.where(eye, sums, 0.0), axis=0, keepdims=True)
        new_sed[k : k + 1, :] = jnp.maximum(spectrum + step_sed * sed_grad, 0.0)


def body(observed, inverse_variance, sed, morph, foot_block, gamma, row_kernel, col_kernel):
    z = Sizes(observed.shape, morph.shape, row_kernel.shape[1])
    sources = morph.shape[1]
    tiles, tile_rows = lax.axis_size("tx"), lax.axis_size("ty")
    chips = tiles // 2
    paired = chips & (chips - 1) == 0

    def hop(value, distance, back=False):
        if paired:
            pairs = [(i, i ^ (2 * distance)) for i in range(tiles)]
        else:
            pairs = [(i, (i + 2 * distance) % tiles) for i in range(tiles)]
            pairs = [(j, i) for i, j in pairs] if back else pairs
        return lax.ppermute(value, "tx", pairs)

    def swap(value):
        return lax.ppermute(value, "tx", [(i, i ^ 1) for i in range(tiles)])

    row = lax.axis_index("ty")
    odd = row & 1

    pairings = [[(i, i + 1) for i in range(start, tile_rows - 1, 2)] for start in (0, 1)]
    pairings = [pairs + [(j, i) for i, j in pairs] for pairs in pairings]
    edges = [1 - odd, odd]
    first = lax.axis_index("tx") * z.per_tile
    place = jnp.stack([first, row, tile_rows - 1 - row, odd]).astype(jnp.int32)

    def edge_rows(value, edge, length):
        start = edge * (value.shape[1] - length)
        size = (value.shape[0], length, value.shape[2])
        return lax.dynamic_slice(value, (0, start, 0), size, allow_negative_indices=False)

    images = [
        jnp.concatenate([edge_rows(v, edge, z.halo) for v in (observed, inverse_variance)])
        for edge in edges
    ]
    sed_tied, images[0], images[1] = lax.optimization_barrier((sed, images[0], images[1]))
    block = pl.pallas_call(
        functools.partial(pack_kernel, z),
        out_shape=jax.ShapeDtypeStruct((sources, z.box + 2 * z.extra, z.box), F32),
        in_specs=[VMEM] * 3,
        out_specs=VMEM,
        compiler_params=params(4),
        name="pack",
    )(morph[0], sed_tied[0], foot_block[0][:, None])
    order = [*range(1, chips, 2), *range(2, chips, 2)]
    blocks = [block] + [hop(block, d) for d in order]
    same = jnp.concatenate(blocks, axis=0)
    other = swap(same)

    table = jnp.concatenate([same[:, : z.bands + 1, 0], other[:, : z.bands + 1, 0]])
    columns = jnp.concatenate([same[:, z.bands], other[:, z.bands]])
    slots = window_slots(z, jnp.concatenate([same, other]), columns, first)
    strips = [edge_rows(slots, edge, z.rim + z.extra) for edge in edges]
    strips = [lax.ppermute(v, "ty", p) for v, p in zip(strips, pairings)]
    images = [lax.ppermute(v, "ty", p) for v, p in zip(images, pairings)]

    matrices, observed_near, weights_near, predicted = inner_call(
        z, place, row_kernel, col_kernel, observed, inverse_variance, slots
    )
    cols_m, grad_m, above_m, below_m, back_m = matrices
    terms = jax.ShapeDtypeStruct((chips * sources, z.box + z.extra, z.box), F32)
    residual, terms_same, terms_other = outer_call(
        z, terms, place, table, same, other, *strips, *images, observed_near, weights_near,
        predicted, cols_m, grad_m, above_m, below_m, back_m,
    )

    chip_terms = terms_same + swap(terms_other)
    per_chip = chip_terms.reshape(chips, sources, z.box + z.extra, z.box)
    received = [per_chip[0]]
    places = list(enumerate(order, 1))[::-1]
    received += [hop(per_chip[at], d, back=True) for at, d in places]
    new_morph, new_sed = pl.pallas_call(
        functools.partial(last_kernel, len(received)),
        out_shape=[
            jax.ShapeDtypeStruct(morph.shape[1:], F32),
            jax.ShapeDtypeStruct(sed.shape[1:], F32),
        ],
        in_specs=[VMEM] * (len(received) + 3),
        out_specs=[VMEM] * 2,
        compiler_params=params(8),
        name="update",
    )(*received, morph[0], sed[0], gamma[0][:, None])
    return residual, new_morph[None], new_sed[None]


def solution(mesh):
    tile = P(None, "ty", "tx")
    source = P("ty", "tx")
    return jax.shard_map(
        body,
        mesh=mesh,
        in_specs=(tile, tile, source, source, source, source, P(), P()),
        out_specs=(tile, source, source),
        check_vma=False,
    )
```

```python
import functools

import jax
import jax.numpy as jnp
from jax import lax
from jax.experimental import pallas as pl
from jax.experimental.pallas import tpu as pltpu
from jax.sharding import PartitionSpec as P

F32 = jnp.float32
BF16 = jnp.bfloat16
VMEM = pl.BlockSpec(memory_space=pltpu.VMEM)
SMEM = pl.BlockSpec(memory_space=pltpu.SMEM)
HBM = pl.BlockSpec(memory_space=pltpu.HBM)
MIB = 1024 * 1024


def params(mebibytes):
    return pltpu.CompilerParams(vmem_limit_bytes=mebibytes * MIB)


def up_to(value, step):
    return -(-value // step) * step


def halves(value):
    high = value.astype(BF16)
    return high, (value - high.astype(F32)).astype(BF16)


def product(left, right):
    dot = functools.partial(jnp.dot, preferred_element_type=F32)
    (lh, ll), (rh, rl) = left, right
    rows = lh.shape[0]
    both = dot(jnp.concatenate([lh, ll], 0), rh)
    return both[:rows] + (dot(lh, rl) + both[rows:])


class Sizes:
    def __init__(self, observed, morph, taps):
        self.bands, self.rows, self.cols = observed
        self.box = morph[-1]
        self.per_tile = self.cols // self.box
        self.taps = taps
        self.reach = (taps - 1) // 2
        self.halo = up_to(self.reach, 8)
        self.rim = up_to(2 * self.reach, 8)
        self.tall = self.rows + 2 * self.halo
        self.near = self.halo + up_to(self.reach, 8)
        self.extra = up_to(self.bands + 1, 8)
        self.slots = 2 * morph[1]


def pack_kernel(z, morph, sed, foot, out):
    row = lax.broadcasted_iota(jnp.int32, (z.extra, z.box), 0)
    for k in range(out.shape[0]):
        info = jnp.where(row == z.bands, foot[k : k + 1, :].astype(F32), 0.0)
        for band in range(z.bands):
            info = jnp.where(row == band, sed[k : k + 1, band : band + 1], info)
        out[k, : z.extra, :] = info
        out[k, z.extra : z.extra + z.box, :] = morph[k]
        out[k, z.extra + z.box :, :] = info


def make_matrices(z, row_ref, col_ref, mats, row_taps, col_taps, cycles, turned):
    cols_m, grad_m, tall_m, above_m, below_m, back_m = [mats[i : i + 2] for i in range(0, 12, 2)]
    box = z.box

    row_taps[...] = jnp.zeros(row_taps.shape, F32)
    col_taps[...] = jnp.zeros(col_taps.shape, F32)
    row_taps[: z.bands, : z.taps] = row_ref[...]
    col_taps[: z.bands, : z.taps] = col_ref[...]

    def cycle(ref, band, shift):
        row = pltpu.roll(jnp.broadcast_to(ref[band : band + 1, :], (8, box)), shift % box, 1)
        spread = jnp.broadcast_to(row[:1, :], (box, box))
        return pltpu.roll(spread, 0, 1, stride=1, stride_axis=0)

    def turn(value, count, shift):
        value = pltpu.roll(value, shift % box, 1)
        return jnp.concatenate([value, value], 0)[:count]

    def tap(count, start, shift):
        at = lax.broadcasted_iota(jnp.int32, (count, box), 1)
        at += start - shift - lax.broadcasted_iota(jnp.int32, (count, box), 0)
        return ((at >= 0) & (at < z.taps)).astype(F32).astype(BF16)

    def cut(value, mask):
        return [half * mask for half in halves(value)]

    def keep(pair, band, value, rows=slice(None), lanes=slice(None)):
        for ref, half in zip(pair, value):
            ref[band, rows, lanes] = half

    as_half = lambda mask: mask.astype(F32).astype(BF16)
    at_row = lax.broadcasted_iota(jnp.int32, (box, box), 0)
    at_lane = lax.broadcasted_iota(jnp.int32, (box, box), 1)
    lower, upper = as_half(at_row >= box // 2), as_half(at_row < box // 2)
    right, left = as_half(at_lane >= box // 2), as_half(at_lane < box // 2)
    none = [jnp.zeros((box, box), BF16)] * 2
    whole = [slice(i * box, (i + 1) * box) for i in range(z.per_tile + 1)]
    col_shift = -z.reach
    tall_shift = -z.halo - z.reach
    above_shift = z.rim - z.halo - z.reach
    below_shift = z.tall - z.near - z.halo - z.rows - z.reach
    back_shift = z.halo - z.reach
    flip_shift = lambda shift: shift + 2 * z.reach + back_shift
    apart = {d: tap(box, d * box, col_shift) for d in (-1, 0, 1)}
    tall_mask = tap(z.tall, 0, tall_shift)
    above_mask = tap(z.near, 0, above_shift)
    below_mask = tap(z.near, 0, below_shift)
    back_masks = [tap(z.rows, start, back_shift) for start in range(0, z.tall, box)]
    for band in range(z.bands):
        cycles[band] = cycle(col_taps, band, col_shift)
        cycles[z.bands + band] = cycle(row_taps, band, back_shift)
    for index in range(2 * z.bands):
        turned[index] = cycles[index].T
    for band in range(z.bands):
        block = {d: cut(cycles[band], apart[d]) for d in apart}
        for i in range(z.per_tile):
            for j in range(z.per_tile):
                keep(cols_m, band, block.get(j - i, none), whole[i], whole[j])
            edge = none
            if i == 0:
                edge = [p + h * lower for p, h in zip(edge, block[1])]
            if i == z.per_tile - 1:
                edge = [p + h * upper for p, h in zip(edge, block[-1])]
            keep(cols_m, band, edge, whole[z.per_tile], whole[i])
        flip = turned[z.bands + band]
        keep(tall_m, band, cut(turn(flip, z.tall, flip_shift(tall_shift)), tall_mask))

    def later_columns(band):
        flipped = {d: cut(turned[band], apart[d]) for d in apart}
        for i in range(z.per_tile):
            for j in range(z.per_tile):
                keep(grad_m, band, flipped.get(j - i, none), whole[i], whole[j])
            edge = none
            if i == 0:
                edge = [p + h * right for p, h in zip(edge, flipped[-1])]
            if i == z.per_tile - 1:
                edge = [p + h * left for p, h in zip(edge, flipped[1])]
            keep(grad_m, band, edge, whole[i], whole[z.per_tile])

    def later_rows(band):
        value, flip = cycles[z.bands + band], turned[z.bands + band]
        for pair, shift, mask in (
            (above_m, above_shift, above_mask),
            (below_m, below_shift, below_mask),
        ):
            part = cut(turn(flip, z.near, flip_shift(shift)), mask)
            keep(pair, band, [h[:, : z.rim] for h in part])
        for index, mask in enumerate(back_masks):
            start = index * box
            size = min(box, z.tall - start)
            part = [h[:, :size] for h in cut(value, mask)]
            keep(back_m, band, part, lanes=slice(start, start + size))

    return later_columns, later_rows


def box_of(z, foot, first):
    place = foot.astype(jnp.int32) - first
    inside = (place >= 0) & (place < z.per_tile)
    near = (place >= -1) & (place <= z.per_tile)
    box = jnp.where(inside, place, z.per_tile)
    low = jnp.where(place == -1, z.box // 2, 0)
    high = jnp.where(place == z.per_tile, z.box // 2, z.box)
    return near, pl.ds(pl.multiple_of(box * z.box, z.box), z.box), low, high


def model_rows(z, place, strips, notes, model, rows):
    first = place[0].astype(F32)
    columns = [note[z.bands : z.bands + 1, :] - first for note in notes]
    for j in range(z.per_tile + 1):
        own = j < z.per_tile
        used = range(z.slots) if own else range(z.slots, 2 * z.slots)
        masks = [(columns[k] == j).astype(F32) for k in used] if own else [1.0] * z.slots
        for band in range(z.bands):
            total = 0.0
            for k, mask in zip(used, masks):
                total += (notes[k][band : band + 1, :] * mask) * strips[k]
            model[band, rows, j * z.box : (j + 1) * z.box] = total


def window_slots(z, rows, columns, first):
    count = columns.shape[0]
    at = columns - first.astype(F32)
    own = ((at >= 0.0) & (at < z.per_tile)).astype(F32)
    lane = lax.broadcasted_iota(jnp.int32, at.shape, 1)
    side = (at == jnp.where(lane >= z.box // 2, -1.0, float(z.per_tile))).astype(F32)
    index = lax.broadcasted_iota(jnp.int32, (count, count, 1), 0)
    earlier = (lax.broadcasted_iota(jnp.int32, (count, count, 1), 1) < index).astype(F32)
    masks = []
    for group in (own, side):
        rank = jnp.sum(earlier * group[None], axis=1)
        masks += [jnp.where(rank == slot, group, 0.0) for slot in range(z.slots)]
    return jnp.stack([jnp.sum(mask[:, None, :] * rows, axis=0) for mask in masks])


def inner_kernel(z, place, row_ref, col_ref, observed, weights, slots, *refs):
    cols_h, cols_l, grad_h, grad_l, above_h, above_l, below_h, below_l, back_h, back_l = refs[:10]
    observed_out, weights_out, predicted = refs[10:13]
    tall_h, tall_l, row_taps, col_taps, cycles, turned, model, blurred, sems = refs[13:]
    copies = [
        pltpu.make_async_copy(observed, observed_out, sems.at[0]),
        pltpu.make_async_copy(weights, weights_out, sems.at[1]),
    ]
    for copy in copies:
        copy.start()
    mats = (cols_h, cols_l, grad_h, grad_l, tall_h, tall_l)
    mats += (above_h, above_l, below_h, below_l, back_h, back_l)
    later_columns, later_rows = make_matrices(
        z, row_ref, col_ref, mats, row_taps, col_taps, cycles, turned
    )
    used = range(2 * z.slots)
    strips = [slots[slot, z.extra : z.extra + z.rows, :] for slot in used]
    notes = [slots[slot, : z.extra, :] for slot in used]
    model_rows(z, place, strips, notes, model, slice(None))
    for band in range(z.bands):
        blurred[band] = product(halves(model[band]), (cols_h[band], cols_l[band]))
        later_columns(band)
    for band in range(z.bands):
        predicted[band] = product((tall_h[band], tall_l[band]), halves(blurred[band]))
        later_rows(band)
    for copy in copies:
        copy.wait()


def outer_kernel(z, place, info, same, other, far_0, far_1, images_0, images_1, *refs):
    observed, weights, predicted = refs[:3]
    cols_m, grad_m, above_m, below_m, back_m = [refs[i : i + 2] for i in range(3, 13, 2)]
    residual_hbm, terms_same, terms_other = refs[13:16]
    residual, model, gradient, backrows, blurred, sems = refs[16:]
    half = same.shape[0]
    odd = place[3]
    for pairing, far in enumerate((far_0, far_1)):
        start = pl.multiple_of(jnp.where(odd == pairing, z.rim, 0), 8)
        rows = pl.ds(start, z.rim)
        upper = pl.ds(pl.multiple_of(jnp.where(odd == pairing, z.extra, 0), 8), z.rim)
        ends = pl.ds(pl.multiple_of(jnp.where(odd == pairing, 0, z.rim), 8), z.extra)
        strips = [far[slot, upper, :] for slot in range(2 * z.slots)]
        notes = [far[slot, ends, :] for slot in range(2 * z.slots)]
        model_rows(z, place, strips, notes, model, rows)
    stores = []
    rest = z.tall - z.near
    middle = slice(z.halo, z.halo + z.rows)
    for band in range(z.bands):
        blurred[band] = product(halves(model[band]), (cols_m[0][band], cols_m[1][band]))
    for band in range(z.bands):
        first = product((above_m[0][band], above_m[1][band]), halves(blurred[band, : z.rim]))
        last = product((below_m[0][band], below_m[1][band]), halves(blurred[band, z.rim :]))
        whole = jnp.concatenate(
            [
                predicted[band, : z.near] + first,
                predicted[band, z.near : rest],
                predicted[band, rest:] + last,
            ],
            0,
        )
        residual[band, middle] = weights[band] * (observed[band] - whole[middle])
        store = pltpu.make_async_copy(
            residual.at[band, middle], residual_hbm.at[band], sems.at[band]
        )
        store.start()
        stores.append(store)
        images = [
            [ref[part + band] for ref in (images_0, images_1)] for part in (0, z.bands)
        ]
        seen, weight = [jnp.where(odd > 0, a, b) for a, b in images]
        residual[band, : z.halo] = weight * (seen - whole[: z.halo])
        seen, weight = [jnp.where(odd > 0, b, a) for a, b in images]
        residual[band, z.halo + z.rows :] = weight * (seen - whole[z.halo + z.rows :])
    for band in range(z.bands):
        backrows[band] = product((back_m[0][band], back_m[1][band]), halves(residual[band]))
    for band in range(z.bands):
        gradient[band] = product(halves(backrows[band]), (grad_m[0][band], grad_m[1][band]))

    lane = lax.broadcasted_iota(jnp.int32, (z.rows, z.box), 1)
    for side, (source, terms) in enumerate(((same, terms_same), (other, terms_other))):

        def step(k, _, side=side, source=source, terms=terms):
            at_info = side * half + k
            near, at, low, high = box_of(z, info[at_info, z.bands], place[0])

            @pl.when(near)
            def _():
                keep = (lane >= low) & (lane < high)
                shape = jnp.where(keep, source[k, z.extra : z.extra + z.rows, :], 0.0)
                total = jnp.zeros((z.rows, z.box), F32)
                for band in range(z.bands):
                    value = gradient[band, :, at]
                    total += info[at_info, band] * value
                    terms[k, z.box + band : z.box + band + 1, :] = jnp.sum(
                        shape * value, axis=0, keepdims=True
                    )
                terms[k, : z.box, :] = jnp.where(keep, total, 0.0)
                unused = terms.shape[1] - z.box - z.bands
                if unused:
                    terms[k, z.box + z.bands :, :] = jnp.zeros((unused, z.box), F32)

            @pl.when(jnp.logical_not(near))
            def _():
                terms[k] = jnp.zeros(terms.shape[1:], F32)

            return 0

        for k in range(half):
            step(k, 0)
    for store in stores:
        store.wait()


def inner_call(z, place, row_kernel, col_kernel, observed, weights, slots):
    sizes = [
        (z.cols + z.box, z.cols),
        (z.cols, z.cols + z.box),
        (z.near, z.rim),
        (z.near, z.rim),
        (z.rows, z.tall),
    ]
    matrices = [jax.ShapeDtypeStruct((z.bands,) + s, BF16) for s in sizes for _ in range(2)]
    *flat, observed, weights, predicted = pl.pallas_call(
        functools.partial(inner_kernel, z),
        out_shape=matrices
        + [jax.ShapeDtypeStruct(observed.shape, F32)] * 2
        + [jax.ShapeDtypeStruct((z.bands, z.tall, z.cols), F32)],
        in_specs=[SMEM] + [VMEM] * 2 + [HBM] * 2 + [VMEM],
        out_specs=[VMEM] * 13,
        scratch_shapes=[pltpu.VMEM((z.bands, z.tall, z.rows), BF16)] * 2
        + [pltpu.VMEM((up_to(z.bands, 8), z.box), F32)] * 2
        + [pltpu.VMEM((2 * z.bands, z.box, z.box), F32)] * 2
        + [
            pltpu.VMEM((z.bands, z.rows, z.cols + z.box), F32),
            pltpu.VMEM((z.bands, z.rows, z.cols), F32),
            pltpu.SemaphoreType.DMA((2,)),
        ],
        compiler_params=params(16),
        cost_estimate=pl.CostEstimate(flops=10**9, bytes_accessed=10**7, transcendentals=0),
        name="inner_rows",
    )(place, row_kernel, col_kernel, observed, weights, slots)
    return [flat[i : i + 2] for i in range(0, 10, 2)], observed, weights, predicted


def outer_call(z, terms, place, table, same, other, far_0, far_1, images_0, images_1, observed,
               weights, predicted, cols_m, grad_m, above_m, below_m, back_m):
    return pl.pallas_call(
        functools.partial(outer_kernel, z),
        out_shape=[jax.ShapeDtypeStruct(observed.shape, F32), terms, terms],
        in_specs=[SMEM] * 2 + [VMEM] * 19,
        out_specs=[HBM, VMEM, VMEM],
        scratch_shapes=[
            pltpu.VMEM((z.bands, z.tall, z.cols), F32),
            pltpu.VMEM((z.bands, 2 * z.rim, z.cols + z.box), F32),
            pltpu.VMEM((z.bands, z.rows, z.cols + z.box), F32),
            pltpu.VMEM((z.bands, z.rows, z.cols), F32),
            pltpu.VMEM((z.bands, 2 * z.rim, z.cols), F32),
            pltpu.SemaphoreType.DMA((z.bands,)),
        ],
        compiler_params=params(12),
        name="whole_step",
    )(
        place, table, same, other, far_0, far_1, images_0, images_1, observed, weights,
        predicted, *cols_m, *grad_m, *above_m, *below_m, *back_m,
    )


def last_kernel(count, *refs):
    received, (morph, sed, gamma, new_morph, new_sed) = refs[:count], refs[count:]
    box = morph.shape[1]
    bands = sed.shape[1]
    for k in range(morph.shape[0]):
        total = received[0][k]
        for ref in received[1:]:
            total += ref[k]
        mine = morph[k]
        spectrum = sed[k : k + 1, :]
        step = gamma[k : k + 1, :]
        step_morph = step / jnp.sum(spectrum * spectrum, axis=1, keepdims=True)
        new_morph[k] = jnp.maximum(mine + step_morph * total[:box], 0.0)
        squares = jnp.sum(jnp.sum(mine * mine, axis=0, keepdims=True), axis=1, keepdims=True)
        step_sed = step / jnp.sqrt(squares)
        sums = jnp.sum(total[box : box + bands], axis=1, keepdims=True)
        eye = lax.broadcasted_iota(jnp.int32, (bands, bands), 0) == lax.broadcasted_iota(
            jnp.int32, (bands, bands), 1
        )
        sed_grad = jnp.sum(jnp.where(eye, sums, 0.0), axis=0, keepdims=True)
        new_sed[k : k + 1, :] = jnp.maximum(spectrum + step_sed * sed_grad, 0.0)


def body(observed, inverse_variance, sed, morph, foot_block, gamma, row_kernel, col_kernel):
    z = Sizes(observed.shape, morph.shape, row_kernel.shape[1])
    sources = morph.shape[1]
    tiles, tile_rows = lax.axis_size("tx"), lax.axis_size("ty")
    chips = tiles // 2
    paired = chips & (chips - 1) == 0

    def hop(value, distance, back=False):
        if paired:
            pairs = [(i, i ^ (2 * distance)) for i in range(tiles)]
        else:
            pairs = [(i, (i + 2 * distance) % tiles) for i in range(tiles)]
            pairs = [(j, i) for i, j in pairs] if back else pairs
        return lax.ppermute(value, "tx", pairs)

    def swap(value):
        return lax.ppermute(value, "tx", [(i, i ^ 1) for i in range(tiles)])

    row = lax.axis_index("ty")
    odd = row & 1

    pairings = [[(i, i + 1) for i in range(start, tile_rows - 1, 2)] for start in (0, 1)]
    pairings = [pairs + [(j, i) for i, j in pairs] for pairs in pairings]
    edges = [1 - odd, odd]
    first = lax.axis_index("tx") * z.per_tile
    place = jnp.stack([first, row, tile_rows - 1 - row, odd]).astype(jnp.int32)

    def edge_rows(value, edge, length):
        start = edge * (value.shape[1] - length)
        size = (value.shape[0], length, value.shape[2])
        return lax.dynamic_slice(value, (0, start, 0), size, allow_negative_indices=False)

    images = [
        jnp.concatenate([edge_rows(v, edge, z.halo) for v in (observed, inverse_variance)])
        for edge in edges
    ]
    sed_tied, images[0], images[1] = lax.optimization_barrier((sed, images[0], images[1]))
    block = pl.pallas_call(
        functools.partial(pack_kernel, z),
        out_shape=jax.ShapeDtypeStruct((sources, z.box + 2 * z.extra, z.box), F32),
        in_specs=[VMEM] * 3,
        out_specs=VMEM,
        compiler_params=params(4),
        name="pack",
    )(morph[0], sed_tied[0], foot_block[0][:, None])
    order = [*range(1, chips, 2), *range(2, chips, 2)]
    blocks = [block] + [hop(block, d) for d in order]
    same = jnp.concatenate(blocks, axis=0)
    other = swap(same)

    table = jnp.concatenate([same[:, : z.bands + 1, 0], other[:, : z.bands + 1, 0]])
    columns = jnp.concatenate([same[:, z.bands], other[:, z.bands]])
    slots = window_slots(z, jnp.concatenate([same, other]), columns, first)
    strips = [edge_rows(slots, edge, z.rim + z.extra) for edge in edges]
    strips = [lax.ppermute(v, "ty", p) for v, p in zip(strips, pairings)]
    images = [lax.ppermute(v, "ty", p) for v, p in zip(images, pairings)]

    matrices, observed_near, weights_near, predicted = inner_call(
        z, place, row_kernel, col_kernel, observed, inverse_variance, slots
    )
    cols_m, grad_m, above_m, below_m, back_m = matrices
    terms = jax.ShapeDtypeStruct((chips * sources, z.box + z.extra, z.box), F32)
    residual, terms_same, terms_other = outer_call(
        z, terms, place, table, same, other, *strips, *images, observed_near, weights_near,
        predicted, cols_m, grad_m, above_m, below_m, back_m,
    )

    chip_terms = terms_same + swap(terms_other)
    per_chip = chip_terms.reshape(chips, sources, z.box + z.extra, z.box)
    received = [per_chip[0]]
    received += [hop(per_chip[at], d, back=True) for at, d in enumerate(order, 1)]
    new_morph, new_sed = pl.pallas_call(
        functools.partial(last_kernel, len(received)),
        out_shape=[
            jax.ShapeDtypeStruct(morph.shape[1:], F32),
            jax.ShapeDtypeStruct(sed.shape[1:], F32),
        ],
        in_specs=[VMEM] * (len(received) + 3),
        out_specs=[VMEM] * 2,
        compiler_params=params(8),
        name="update",
    )(*received, morph[0], sed[0], gamma[0][:, None])
    return residual, new_morph[None], new_sed[None]


def solution(mesh):
    tile = P(None, "ty", "tx")
    source = P("ty", "tx")
    return jax.shard_map(
        body,
        mesh=mesh,
        in_specs=(tile, tile, source, source, source, source, P(), P()),
        out_specs=(tile, source, source),
        check_vma=False,
    )
```
